32 devices in a mesh: branch: 4 (over x, core), dp: 4 (over z), mp: 2 (over y).
Axes of the slice: x: 2, y: 2, z: 4, core: 2. Of those that a mesh axis runs over, the one named last changes fastest.
Arguments:
- hidden_in: bfloat16 [2048, 7168], P(('branch', 'dp'), 'mp'), parts along dimension 0, may hold values from -54 to 54
- embed_in: bfloat16 [2048, 7168], P(('branch', 'dp'), 'mp'), parts along dimension 0, may hold values from -54 to 54
- hidden_gain: float32 [28672], P(('branch', 'mp')), parts along dimension 0, may hold values from 0.1 to 1.9
- embed_gain: float32 [28672], P(('branch', 'mp')), parts along dimension 0, may hold values from 0.1 to 1.9
- w_proj_hidden: bfloat16 [28672, 7168], P(('branch', 'mp'), 'dp'), parts along dimension 0, may hold values from -0.10022297 to 0.10022297
- w_proj_embed: bfloat16 [28672, 7168], P(('branch', 'mp'), 'dp'), parts along dimension 0, may hold values from -0.10022297 to 0.10022297
- attn_gain: float32 [28672], P(('branch', 'dp')), parts along dimension 0, may hold values from 0.1 to 1.9
- w_latent: bfloat16 [28672, 2112], P(('branch', 'dp')), parts along dimension 0, may hold values from -0.0625 to 0.0625
- q_gain: float32 [6144], P('branch'), parts along dimension 0, may hold values from 0.1 to 1.9
- kv_gain: float32 [2048], P('branch'), parts along dimension 0, may hold values from 0.1 to 1.9
Outputs:
- mtp_hidden: bfloat16 [2048, 7168], P(('branch', 'mp'), 'dp'), parts along dimension 0
- q_latent: bfloat16 [2048, 1536], P(('branch', 'mp', 'dp')), parts along dimension 0
- kv_latent: bfloat16 [2048, 512], P(('branch', 'mp', 'dp')), parts along dimension 0
- key_rope: bfloat16 [2048, 64], P(('branch', 'mp', 'dp')), parts along dimension 0
The draws below stay inside these ranges and needn't reach their ends.
There are 4 independent parts, one for each index of `branch`. The reference program is written for one: setup_inputs(seed, part) draws one part's arguments, and reference() takes and returns one part's arrays. A program takes and returns all parts, laid end to end along the dimension named above; each array names one. Nothing has to cross between parts.
All inputs are finite; a program needn't handle non-finite values.
Results may differ from the reference program's by a relative error of at most 0.03.
Values may be sent and summed in bfloat16 or wider, within the bound.
No kernel may reach another device: no remote copies, remote signals or barrier semaphores. Data moves between devices by JAX's collectives and lax.ppermute only.
A program may use at most 128 MiB of HBM per device.

```python
import math
import jax
import jax.numpy as jnp
from jax import lax

D = 7168
Q_LAT = 1536
KV_LAT = 512
LENGTH = 2048
TOKENS = 512
LAT = 2112
N_MP = 2


def entry_field(key):
    base_key, power_key, row_key = jax.random.split(key, 3)
    columns = jnp.arange(D, dtype=jnp.float32) / D
    profile_power = jax.random.uniform(power_key, (TOKENS, 1), jnp.float32, 0.3, 1.3)
    base_values = jax.random.truncated_normal(base_key, -4.0, 4.0, (TOKENS, D), jnp.float32)
    row_scale = jnp.exp(jax.random.uniform(row_key, (TOKENS, 1), jnp.float32, math.log(0.3), math.log(3.0)))
    profile = jnp.exp(profile_power * math.log(10.0) * (columns[None, :] - 0.5))
    return (base_values * row_scale * profile).astype(jnp.bfloat16)


def proj_matrix(key):
    rows_in = jnp.arange(D, dtype=jnp.float32) / D
    cols_out = jnp.arange(D, dtype=jnp.float32) / D
    base_values = jax.random.truncated_normal(key, -4.0, 4.0, (D, D), jnp.float32)
    row_factor = jnp.exp(math.log(4.0) * rows_in)[:, None]
    col_factor = jnp.exp(math.log(3.0) * (cols_out - 0.5))[None, :]
    return (base_values * (0.43 / math.sqrt(2.0 * D)) * row_factor * col_factor).astype(jnp.bfloat16)


def draw_hidden_in(key, part):
    return entry_field(jax.random.fold_in(key, 11))


def draw_embed_in(key, part):
    return entry_field(jax.random.fold_in(key, 23))


def draw_w_proj_hidden(key, part):
    return proj_matrix(jax.random.fold_in(key, 37))


def draw_w_proj_embed(key, part):
    return proj_matrix(jax.random.fold_in(key, 41))


def block_levels(own_key, shape, cuts, least, largest):
    level = 1.0
    for dim, blocks in cuts:
        steps = jax.random.uniform(jax.random.fold_in(jax.random.fold_in(own_key, 6), dim), (blocks,), jnp.float32, least / len(cuts), largest / len(cuts))
        level = level * jnp.repeat(jnp.exp(steps), shape[dim] // blocks).reshape((-1,) + (1,) * (len(shape) - 1 - dim))
    return level


def normal_values(rng, dims, scale, bound, cuts=(), kind=jnp.bfloat16):
    level = block_levels(rng, dims, cuts, -0.22, 0.18) if cuts else 1.0
    result = jax.random.normal(rng, dims, jnp.float32) * scale * level
    return jnp.minimum(jnp.maximum(result, -bound), bound).astype(kind)


def setup_inputs(seed: int = 0, part: int = 0) -> dict:
    splits = jax.random.split(jax.random.key(seed), 11)
    own_keys = jax.random.split(jax.random.fold_in(splits[10], part), 11)
    return {
        "hidden_in": draw_hidden_in(jax.random.fold_in(jax.random.fold_in(splits[10], part), 71), part),
        "embed_in": draw_embed_in(jax.random.fold_in(jax.random.fold_in(splits[10], part), 71), part),
        "hidden_gain": jnp.clip(1.0 + 0.18 * jax.random.normal(own_keys[2], (D,), jnp.float32), 0.1, 1.9),
        "embed_gain": jnp.clip(1.0 + 0.18 * jax.random.normal(own_keys[3], (D,), jnp.float32), 0.1, 1.9),
        "w_proj_hidden": draw_w_proj_hidden(jax.random.fold_in(jax.random.fold_in(splits[10], part), 71), part),
        "w_proj_embed": draw_w_proj_embed(jax.random.fold_in(jax.random.fold_in(splits[10], part), 71), part),
        "attn_gain": jnp.clip(1.0 + 0.18 * jax.random.normal(own_keys[6], (D,), jnp.float32), 0.1, 1.9),
        "w_latent": normal_values(own_keys[7], (D, LAT), D ** -0.5, 0.0625, ((0, 4),)),
        "q_gain": jnp.clip(1.0 + 0.18 * jax.random.normal(own_keys[8], (Q_LAT,), jnp.float32), 0.1, 1.9),
        "kv_gain": jnp.clip(1.0 + 0.18 * jax.random.normal(own_keys[9], (KV_LAT,), jnp.float32), 0.1, 1.9),
    }


epsilon = 1e-06

def inverse_rms(squares_total, width):
    return lax.rsqrt(squares_total / width + epsilon)

def latent_norm(part, gain):
    scale_rows = inverse_rms(lax.optimization_barrier(jnp.sum(part * part, axis=1)), part.shape[1])
    return (part * scale_rows[:, None] * gain[None, :]).astype(jnp.bfloat16)

def rotate_keys(rope_part, positions):
    half_width = rope_part.shape[1] // 2
    frequency = jnp.exp(jnp.arange(half_width, dtype=jnp.float32) * (-2.0 * math.log(10000.0) / rope_part.shape[1]))
    angle_grid = positions.astype(jnp.float32)[:, None] * frequency[None, :]
    cosine = jnp.cos(angle_grid)
    sine_grid = jnp.sin(angle_grid)
    lower_half = rope_part[:, :half_width]
    upper_half = rope_part[:, half_width:]
    return jnp.concatenate([lower_half * cosine - upper_half * sine_grid, lower_half * sine_grid + upper_half * cosine], axis=1)

def reference(hidden_in, embed_in, hidden_gain, embed_gain, w_proj_hidden, w_proj_embed, attn_gain, w_latent, q_gain, kv_gain):
    hidden_wide = hidden_in.astype(jnp.float32)
    embed_wide = embed_in.astype(jnp.float32)
    hidden_norm = (hidden_wide * inverse_rms(lax.optimization_barrier(jnp.sum(hidden_wide * hidden_wide, axis=1)), D)[:, None] * hidden_gain[None, :]).astype(jnp.bfloat16)
    embed_norm = (embed_wide * inverse_rms(lax.optimization_barrier(jnp.sum(embed_wide * embed_wide, axis=1)), D)[:, None] * embed_gain[None, :]).astype(jnp.bfloat16)
    shard_width = D // N_MP

    def add_shard(shard_index, running):
        first_col = (shard_index * shard_width).astype(jnp.int32)
        hidden_cols = lax.dynamic_slice_in_dim(hidden_norm, first_col, shard_width, 1)
        embed_cols = lax.dynamic_slice_in_dim(embed_norm, first_col, shard_width, 1)
        hidden_block = lax.dynamic_slice_in_dim(w_proj_hidden, first_col, shard_width, 0)
        embed_block = lax.dynamic_slice_in_dim(w_proj_embed, first_col, shard_width, 0)
        shard_term = jnp.dot(hidden_cols, hidden_block, preferred_element_type=jnp.float32) + jnp.dot(embed_cols, embed_block, preferred_element_type=jnp.float32)
        rounded = lax.optimization_barrier(shard_term.astype(jnp.bfloat16))
        return running + rounded.astype(jnp.float32)
    proj_sum = lax.fori_loop(0, N_MP, add_shard, jnp.zeros((TOKENS, D), jnp.float32))
    mtp_hidden = lax.optimization_barrier(proj_sum.astype(jnp.bfloat16))
    proj_wide = mtp_hidden.astype(jnp.float32)
    attn_scale = inverse_rms(lax.optimization_barrier(jnp.sum(proj_wide * proj_wide, axis=1)), D)
    normed_rows = (proj_wide * attn_gain[None, :]).astype(jnp.bfloat16)
    latent = jnp.dot(normed_rows, w_latent, preferred_element_type=jnp.float32) * attn_scale[:, None]
    positions = jnp.arange(TOKENS, dtype=jnp.int32) % LENGTH
    q_latent = latent_norm(latent[:, :Q_LAT], q_gain)
    kv_latent = latent_norm(latent[:, Q_LAT:Q_LAT + KV_LAT], kv_gain)
    key_rope = rotate_keys(latent[:, Q_LAT + KV_LAT:], positions).astype(jnp.bfloat16)
    return (mtp_hidden, q_latent, kv_latent, key_rope)
```

```python
import math

import jax
import jax.numpy as jnp
from jax import lax
from jax.experimental import pallas as pl
from jax.experimental.pallas import tpu as pltpu
from jax.sharding import PartitionSpec as P

D = 7168
Q_LAT = 1536
KV_LAT = 512
LENGTH = 2048
LANES = 128
VMEM_BYTES = 48 * 1024 * 1024

epsilon = 1e-06


def inverse_rms(squares_total, width):
    return lax.rsqrt(squares_total / width + epsilon)


def latent_norm(part, gain):
    scale_rows = inverse_rms(jnp.sum(part * part, axis=1), part.shape[1])
    return (part * scale_rows[:, None] * gain[None, :]).astype(jnp.bfloat16)


def rope_tables(width, positions):
    half_width = width // 2
    frequency = jnp.exp(
        jnp.arange(half_width, dtype=jnp.float32) * (-2.0 * math.log(10000.0) / width)
    )
    angle_grid = positions.astype(jnp.float32)[:, None] * frequency[None, :]
    return jnp.cos(angle_grid), jnp.sin(angle_grid)


def rotate_keys(rope_part, cosine, sine_grid):
    half_width = rope_part.shape[1] // 2
    lower_half = rope_part[:, :half_width]
    upper_half = rope_part[:, half_width:]
    return jnp.concatenate(
        [
            lower_half * cosine - upper_half * sine_grid,
            lower_half * sine_grid + upper_half * cosine,
        ],
        axis=1,
    )


def block_of(size, most):
    best = LANES
    for width in range(LANES, most + 1, LANES):
        if size % width == 0:
            best = width
    return best


def project(groups, scales, hidden_gain, embed_gain, w_hidden, w_embed, own_first=None):
    depth, width = w_hidden.shape
    step = block_of(depth, 512)
    steps = depth // step
    counts = [len(group) for group in groups]
    arrays = [array for group in groups for array in group]
    rows = [group[0].shape[0] for group in groups]
    total = sum(rows)
    swaps = own_first is not None

    def body(*refs):
        refs = list(refs)
        flag = refs.pop(0) if swaps else None
        hidden_refs = refs[: len(arrays)]
        embed_refs = refs[len(arrays) : 2 * len(arrays)]
        scale_ref, hgain_ref, egain_ref, wh_ref, we_ref = refs[2 * len(arrays) : 2 * len(arrays) + 5]
        outs = refs[2 * len(arrays) + 5 : -1]
        acc = refs[-1]
        index = pl.program_id(0)

        @pl.when(index == 0)
        def _():
            acc[...] = jnp.zeros_like(acc)

        def normed(sources, gain_ref, column):
            parts = []
            at = 0
            for count in counts:
                value = sources[at][...].astype(jnp.float32)
                for other in sources[at + 1 : at + count]:
                    value = value + other[...].astype(jnp.float32)
                at += count
                parts.append(value)
            whole = parts[0] if len(parts) == 1 else jnp.concatenate(parts, axis=0)
            return (whole * scale_ref[:, column : column + 1] * gain_ref[...]).astype(jnp.bfloat16)

        acc[...] += jnp.dot(
            normed(hidden_refs, hgain_ref, 0), wh_ref[...], preferred_element_type=jnp.float32
        ) + jnp.dot(
            normed(embed_refs, egain_ref, 1), we_ref[...], preferred_element_type=jnp.float32
        )

        @pl.when(index == steps - 1)
        def _():
            if swaps:
                first = acc[: rows[0], :].astype(jnp.bfloat16)
                second = acc[rows[0] :, :].astype(jnp.bfloat16)
                keep = flag[0] == 1
                outs[0][...] = jnp.where(keep, first, second)
                outs[1][...] = jnp.where(keep, second, first)
            else:
                outs[0][...] = acc[...].astype(jnp.bfloat16)

    in_specs = [pl.BlockSpec(memory_space=pltpu.SMEM)] if swaps else []
    for array in arrays:
        in_specs.append(pl.BlockSpec((array.shape[0], step), lambda k: (0, k)))
    for array in arrays:
        in_specs.append(pl.BlockSpec((array.shape[0], step), lambda k: (0, steps + k)))
    in_specs += [
        pl.BlockSpec((total, 2), lambda k: (0, 0)),
        pl.BlockSpec((1, step), lambda k: (0, k)),
        pl.BlockSpec((1, step), lambda k: (0, k)),
        pl.BlockSpec((step, width), lambda k: (k, 0)),
        pl.BlockSpec((step, width), lambda k: (k, 0)),
    ]
    out_rows = rows if swaps else [total]
    result = pl.pallas_call(
        body,
        grid=(steps,),
        in_specs=in_specs,
        out_specs=[pl.BlockSpec((r, width), lambda k: (0, 0)) for r in out_rows],
        out_shape=[jax.ShapeDtypeStruct((r, width), jnp.bfloat16) for r in out_rows],
        scratch_shapes=[pltpu.VMEM((total, width), jnp.float32)],
        compiler_params=pltpu.CompilerParams(vmem_limit_bytes=VMEM_BYTES),
        cost_estimate=pl.CostEstimate(
            flops=4 * total * depth * width, bytes_accessed=4 * depth * width, transcendentals=0
        ),
        name="project",
    )(
        *([own_first] if swaps else []),
        *arrays,
        *arrays,
        scales,
        hidden_gain[None, :],
        embed_gain[None, :],
        w_hidden,
        w_embed,
    )
    return result if swaps else result[0]


def latent_partial(own, received, gain, w_latent):
    rows, width = own.shape
    lat = w_latent.shape[1]
    padded = -(-(lat + 2) // LANES) * LANES
    edge = padded - LANES
    step = block_of(width, 256)
    steps = width // step

    def body(own_ref, received_ref, gain_ref, w_ref, mtp_ref, lat_ref, acc, squares):
        index = pl.program_id(0)

        @pl.when(index == 0)
        def _():
            acc[...] = jnp.zeros_like(acc)
            squares[...] = jnp.zeros_like(squares)

        mtp = (own_ref[...].astype(jnp.float32) + received_ref[...].astype(jnp.float32)).astype(
            jnp.bfloat16
        )
        mtp_ref[...] = mtp
        wide = mtp.astype(jnp.float32)
        squares[...] += jnp.sum(wide * wide, axis=1, keepdims=True)
        normed = (wide * gain_ref[...]).astype(jnp.bfloat16)
        acc[:, :lat] += jnp.dot(normed, w_ref[...], preferred_element_type=jnp.float32)

        @pl.when(index == steps - 1)
        def _():
            lat_ref[:, :edge] = acc[:, :edge].astype(jnp.bfloat16)
            column = lax.broadcasted_iota(jnp.int32, (rows, LANES), 1)
            total = squares[...]
            high = total.astype(jnp.bfloat16).astype(jnp.float32)
            tail = jnp.where(column == lat - edge, high, jnp.where(column == lat - edge + 1, total - high, 0.0))
            tail = jnp.where(column < lat - edge, acc[:, edge:], tail)
            lat_ref[:, edge:] = tail.astype(jnp.bfloat16)

    return pl.pallas_call(
        body,
        grid=(steps,),
        in_specs=[
            pl.BlockSpec((rows, step), lambda k: (0, k)),
            pl.BlockSpec((rows, step), lambda k: (0, k)),
            pl.BlockSpec((1, step), lambda k: (0, k)),
            pl.BlockSpec((step, lat), lambda k: (k, 0)),
        ],
        out_specs=[
            pl.BlockSpec((rows, step), lambda k: (0, k)),
            pl.BlockSpec((rows, padded), lambda k: (0, 0)),
        ],
        out_shape=[
            jax.ShapeDtypeStruct((rows, width), jnp.bfloat16),
            jax.ShapeDtypeStruct((rows, padded), jnp.bfloat16),
        ],
        scratch_shapes=[
            pltpu.VMEM((rows, padded), jnp.float32),
            pltpu.VMEM((rows, 1), jnp.float32),
        ],
        compiler_params=pltpu.CompilerParams(vmem_limit_bytes=VMEM_BYTES),
        cost_estimate=pl.CostEstimate(
            flops=2 * rows * width * lat, bytes_accessed=2 * width * lat, transcendentals=0
        ),
        name="latent_partial",
    )(own, received, gain[None, :], w_latent)


def finish(base, late, q_gain, kv_gain, cosine, sine_grid):
    rows = base.shape[0]
    lat = Q_LAT + KV_LAT
    rope = 2 * cosine.shape[1]

    def body(base_ref, *refs):
        late_refs = refs[: len(late)]
        qg_ref, kg_ref, cos_ref, sin_ref, q_ref, kv_ref, rope_ref, total = refs[len(late) :]
        total[...] = base_ref[...]
        for (at, array), ref in zip(late, late_refs, strict=True):
            total[at : at + array.shape[0], :] += ref[...].astype(jnp.float32)
        whole = total[...]
        squares = whole[:, lat + rope : lat + rope + 1] + whole[:, lat + rope + 1 : lat + rope + 2]
        latent = whole * inverse_rms(squares, D)
        q = latent[:, :Q_LAT]
        kv = latent[:, Q_LAT:lat]
        q_scale = inverse_rms(jnp.sum(q * q, axis=1, keepdims=True), Q_LAT)
        kv_scale = inverse_rms(jnp.sum(kv * kv, axis=1, keepdims=True), KV_LAT)
        q_ref[...] = (q * q_scale * qg_ref[...]).astype(jnp.bfloat16)
        kv_ref[...] = (kv * kv_scale * kg_ref[...]).astype(jnp.bfloat16)
        keys = rotate_keys(latent[:, lat : lat + rope], cos_ref[...], sin_ref[...])
        rope_ref[...] = keys.astype(jnp.bfloat16)

    return pl.pallas_call(
        body,
        out_shape=[
            jax.ShapeDtypeStruct((rows, Q_LAT), jnp.bfloat16),
            jax.ShapeDtypeStruct((rows, KV_LAT), jnp.bfloat16),
            jax.ShapeDtypeStruct((rows, rope), jnp.bfloat16),
        ],
        scratch_shapes=[pltpu.VMEM(base.shape, jnp.float32)],
        compiler_params=pltpu.CompilerParams(vmem_limit_bytes=VMEM_BYTES),
        name="finish",
    )(base, *[array for _, array in late], q_gain[None, :], kv_gain[None, :], cosine, sine_grid)


def rounds_of(pairs):
    lists = []
    for source, target in pairs:
        for chosen in lists:
            if all(source != s and target != t for s, t in chosen):
                chosen.append((source, target))
                break
        else:
            lists.append([(source, target)])
    return lists


def shards_line(
    hidden_in, embed_in, hidden_gain, embed_gain, w_hidden, w_embed, attn_gain, w_latent, q_gain, kv_gain
):
    line = lax.axis_size("dp")
    shard = hidden_in.shape[0]
    rows_out = shard // 2
    cuts = ((0, rows_out), (rows_out, shard))
    me = lax.axis_index("dp")
    mine = lax.axis_index("mp")
    last = line - 1

    def owner(s):
        return s // 2

    def device(d, m):
        return d * 2 + m

    pieces = [
        jnp.concatenate([hidden_in[low:high], embed_in[low:high]], axis=1) for low, high in cuts
    ]

    hidden_wide = hidden_in.astype(jnp.float32)
    embed_wide = embed_in.astype(jnp.float32)
    sums = jnp.stack(
        [jnp.sum(hidden_wide * hidden_wide, axis=1), jnp.sum(embed_wide * embed_wide, axis=1)], axis=1
    )
    sums = sums + lax.ppermute(sums, "mp", [(0, 1), (1, 0)])
    scale_all = inverse_rms(lax.all_gather(sums, "dp", axis=0, tiled=True), D)

    def scale_rows(s, low, high):
        return lax.dynamic_slice_in_dim(scale_all, s * shard + low, high - low, 0)

    def rows(groups, scales, own_first=None):
        return project(groups, scales, hidden_gain, embed_gain, w_hidden, w_embed, own_first)

    def to_owner(value, senders):
        pairs = [(device(d, 1 - m), device(d, m)) for d, m in senders]
        return lax.ppermute(value, ("dp", "mp"), pairs)

    def shard_of(k, d):
        return sorted({s for s in (d - k, d + k) if 0 <= s < line})

    def senders_of(k):
        return [(d, owner(s)) for d in range(line) for s in shard_of(k, d)]

    def send_latent(k, low, value):
        pairs = []
        for d in range(line):
            for s in shard_of(k, d):
                target = (s % 2) * 2 + low // rows_out
                if target != d:
                    pairs.append((device(d, owner(s)), device(target, owner(s))))
        return [lax.ppermute(value, ("dp", "mp"), chosen) for chosen in rounds_of(pairs)]

    mtp_steps = []
    own_steps = []
    early = []
    late = []
    forward = list(pieces)
    backward = list(pieces)
    got = rows([[piece] for piece in pieces], scale_rows(me, 0, shard))
    mtp, lat = latent_partial(got, to_owner(got, senders_of(0)), attn_gain, w_latent)
    mtp_steps.append(mtp)
    own_steps.append(lat)
    for low, high in cuts:
        early += [(low % rows_out, array) for array in send_latent(0, low, lat[low:high])]
    for k in range(1, line):
        forward = [lax.ppermute(x, "dp", [(i, i + 1) for i in range(k - 1, last)]) for x in forward]
        backward = [lax.ppermute(x, "dp", [(i + 1, i) for i in range(0, line - k)]) for x in backward]
        mtps = []
        lats = []
        for (low, high), ahead, back in zip(cuts, forward, backward, strict=True):
            if k < line // 2:
                first = jnp.where(me >= 1, owner(me - 1) == mine, owner(me + 1) != mine)
                scales = jnp.concatenate(
                    [
                        scale_rows(jnp.maximum(me - k, 0), low, high),
                        scale_rows(jnp.minimum(me + k, last), low, high),
                    ],
                    axis=0,
                )
                got, other = rows([[ahead], [back]], scales, first.astype(jnp.int32)[None])
            else:
                got = rows([[ahead, back]], scale_rows(jnp.where(me >= k, me - k, jnp.minimum(me + k, last)), low, high))
                other = got
            mtp, lat = latent_partial(got, to_owner(other, senders_of(k)), attn_gain, w_latent)
            mtps.append(mtp)
            lats.append(lat)
            arrays = [(low % rows_out, array) for array in send_latent(k, low, lat)]
            if k == last:
                late += arrays
            else:
                early += arrays
        mtp_steps.append(jnp.concatenate(mtps, axis=0))
        own_steps.append(jnp.concatenate(lats, axis=0) if k < last else None)

    halves = []
    for offset in range(2):
        distance = jnp.abs(me - (2 * mine + offset))
        halves.append(lax.select_n(distance, *mtp_steps))
    mtp_hidden = jnp.concatenate(halves, axis=0)

    distance = jnp.abs(me - (2 * mine + me // 2))
    whole = lax.select_n(distance, *own_steps[:-1])
    base = lax.dynamic_slice_in_dim(whole, (me % 2) * rows_out, rows_out, 0).astype(jnp.float32)
    for at, array in early:
        base = base + jnp.pad(array.astype(jnp.float32), ((at, rows_out - at - array.shape[0]), (0, 0)))
    first_token = (mine * line + me) * rows_out
    positions = (first_token + jnp.arange(rows_out, dtype=jnp.int32)) % LENGTH
    cosine, sine_grid = rope_tables(w_latent.shape[1] - Q_LAT - KV_LAT, positions)
    q_latent, kv_latent, key_rope = finish(base, late, q_gain, kv_gain, cosine, sine_grid)
    return (mtp_hidden, q_latent, kv_latent, key_rope)


def shards_any(
    hidden_in, embed_in, hidden_gain, embed_gain, w_hidden, w_embed, attn_gain, w_latent, q_gain, kv_gain
):
    hidden_wide = hidden_in.astype(jnp.float32)
    embed_wide = embed_in.astype(jnp.float32)
    entry_sums = lax.psum(
        (jnp.sum(hidden_wide * hidden_wide, axis=1), jnp.sum(embed_wide * embed_wide, axis=1)), "mp"
    )
    hidden_norm = (hidden_wide * inverse_rms(entry_sums[0], D)[:, None] * hidden_gain[None, :]).astype(jnp.bfloat16)
    embed_norm = (embed_wide * inverse_rms(entry_sums[1], D)[:, None] * embed_gain[None, :]).astype(jnp.bfloat16)
    hidden_all = lax.all_gather(hidden_norm, "dp", axis=0, tiled=True)
    embed_all = lax.all_gather(embed_norm, "dp", axis=0, tiled=True)
    tok_share = hidden_all.shape[0] // lax.axis_size("mp")
    proj_sum = lax.psum_scatter(
        (
            jnp.dot(hidden_all, w_hidden, preferred_element_type=jnp.float32)
            + jnp.dot(embed_all, w_embed, preferred_element_type=jnp.float32)
        ).astype(jnp.bfloat16),
        "mp",
        scatter_dimension=0,
        tiled=True,
    )
    mtp_hidden = lax.optimization_barrier(proj_sum)
    proj_wide = mtp_hidden.astype(jnp.float32)
    normed_rows = (proj_wide * attn_gain[None, :]).astype(jnp.bfloat16)
    partial_latent = jnp.dot(normed_rows, w_latent, preferred_element_type=jnp.float32)
    rows_out = tok_share // lax.axis_size("dp")
    square_total = lax.psum(jnp.sum(proj_wide * proj_wide, axis=1), "dp")
    latent_sum = lax.psum_scatter(
        partial_latent.astype(jnp.bfloat16), "dp", scatter_dimension=0, tiled=True
    ).astype(jnp.float32)
    first_own = lax.axis_index("dp") * rows_out
    square_sum = lax.dynamic_slice_in_dim(square_total, first_own, rows_out, 0)
    latent = latent_sum * inverse_rms(square_sum, D)[:, None]
    first_token = lax.axis_index("mp") * tok_share + first_own
    positions = (first_token + jnp.arange(rows_out, dtype=jnp.int32)) % LENGTH
    q_latent = latent_norm(latent[:, :Q_LAT], q_gain)
    kv_latent = latent_norm(latent[:, Q_LAT : Q_LAT + KV_LAT], kv_gain)
    rope_part = latent[:, Q_LAT + KV_LAT :]
    key_rope = rotate_keys(rope_part, *rope_tables(rope_part.shape[1], positions)).astype(jnp.bfloat16)
    return (mtp_hidden, q_latent, kv_latent, key_rope)


def solution(mesh):
    placed = (
        P(("branch", "dp"), "mp"),
        P(("branch", "dp"), "mp"),
        P(("branch", "mp")),
        P(("branch", "mp")),
        P(("branch", "mp"), "dp"),
        P(("branch", "mp"), "dp"),
        P(("branch", "dp")),
        P(("branch", "dp"), None),
        P("branch"),
        P("branch"),
    )
    in_line = mesh.shape["dp"] == 4 and mesh.shape["mp"] == 2
    return jax.shard_map(
        shards_line if in_line else shards_any,
        mesh=mesh,
        in_specs=placed,
        out_specs=(
            P(("branch", "mp"), "dp"),
            P(("branch", "mp", "dp"), None),
            P(("branch", "mp", "dp"), None),
            P(("branch", "mp", "dp"), None),
        ),
        check_vma=False,
    )
```

```python
import math

import jax
import jax.numpy as jnp
from jax import lax
from jax.experimental import pallas as pl
from jax.experimental.pallas import tpu as pltpu
from jax.sharding import PartitionSpec as P

D = 7168
Q_LAT = 1536
KV_LAT = 512
LENGTH = 2048
LANES = 128
TERMS = 3
VMEM_BYTES = 9 * 1024 * 1024

epsilon = 1e-06


def inverse_rms(squares_total, width):
    return lax.rsqrt(squares_total / width + epsilon)


def latent_norm(part, gain):
    scale_rows = inverse_rms(jnp.sum(part * part, axis=1), part.shape[1])
    return (part * scale_rows[:, None] * gain[None, :]).astype(jnp.bfloat16)


def rope_tables(width, positions):
    half_width = width // 2
    frequency = jnp.exp(
        jnp.arange(half_width, dtype=jnp.float32) * (-2.0 * math.log(10000.0) / width)
    )
    angle_grid = positions.astype(jnp.float32)[:, None] * frequency[None, :]
    return jnp.cos(angle_grid), jnp.sin(angle_grid)


def rotate_keys(rope_part, cosine, sine_grid):
    half_width = rope_part.shape[1] // 2
    lower_half = rope_part[:, :half_width]
    upper_half = rope_part[:, half_width:]
    return jnp.concatenate(
        [
            lower_half * cosine - upper_half * sine_grid,
            lower_half * sine_grid + upper_half * cosine,
        ],
        axis=1,
    )


def resident(array):
    return pltpu.with_memory_space_constraint(array, pltpu.VMEM)


def after(value, *others):
    return lax.optimization_barrier((value, *others))[0]


VMEM = pl.BlockSpec(memory_space=pltpu.VMEM)
NO_COST = pl.CostEstimate(flops=0, bytes_accessed=0, transcendentals=0)
SOME_COST = pl.CostEstimate(flops=0, bytes_accessed=15_000_000, transcendentals=0)
MORE_COST = pl.CostEstimate(flops=0, bytes_accessed=100_000_000, transcendentals=0)


def kernel(body, name, inputs, outputs, scratch=(), cost=NO_COST):
    return pl.pallas_call(
        body,
        in_specs=[VMEM] * len(inputs),
        out_specs=[VMEM] * len(outputs),
        out_shape=[jax.ShapeDtypeStruct(shape, kind) for shape, kind in outputs],
        scratch_shapes=list(scratch),
        compiler_params=pltpu.CompilerParams(vmem_limit_bytes=VMEM_BYTES),
        cost_estimate=cost,
        name=name,
    )(*inputs)


def enter(hidden, embed, cuts):
    rows, depth = hidden.shape

    def body(hidden_ref, embed_ref, *outs):
        sums = []
        for column, ref in enumerate((hidden_ref, embed_ref)):
            for (low, high), out in zip(cuts[:-1], outs, strict=False):
                out[:, column * depth : (column + 1) * depth] = ref[low:high, :]
            wide = ref[...].astype(jnp.float32)
            sums.append(jnp.sum(wide * wide, axis=1, keepdims=True))
        lane = lax.broadcasted_iota(jnp.int32, (rows, LANES), 1)
        outs[-1][...] = jnp.where(lane == 0, sums[0], jnp.where(lane == 1, sums[1], 0.0))

    outputs = [((high - low, 2 * depth), jnp.bfloat16) for low, high in cuts[:-1]]
    *pieces, sums = kernel(body, "enter", [hidden, embed], outputs + [((rows, LANES), jnp.float32)])
    return pieces, sums


def pack(hidden, embed, sums, other_sums, low):
    rows, depth = hidden.shape
    height = rows - low

    def body(hidden_ref, embed_ref, sums_ref, other_ref, piece_ref, total_ref):
        total = sums_ref[...] + other_ref[...]
        total_ref[...] = total
        piece_ref[:, :depth] = hidden_ref[low:, :]
        piece_ref[:, depth : 2 * depth] = embed_ref[low:, :]
        lane = lax.broadcasted_iota(jnp.int32, (height, LANES), 1)
        spare = jnp.zeros((height, LANES), jnp.float32)
        at = 0
        for start in range(0, rows, height):
            for column in range(2):
                rest = total[start : start + height, column : column + 1]
                for _ in range(TERMS):
                    term = rest.astype(jnp.bfloat16).astype(jnp.float32)
                    rest = rest - term
                    spare = jnp.where(lane == at, term, spare)
                    at += 1
        piece_ref[:, 2 * depth :] = spare.astype(jnp.bfloat16)

    outputs = [((height, 2 * depth + LANES), jnp.bfloat16), (sums.shape, jnp.float32)]
    return kernel(body, "pack", [hidden, embed, sums, other_sums], outputs)


def project(groups, weights, own_first=None, cost=NO_COST):
    hidden_gain, embed_gain, w_hidden, w_embed = weights
    depth, width = w_hidden.shape
    packed = [isinstance(group[1], list) for group in groups]
    inputs = []
    for arrays, sums, _ in groups:
        inputs += [*arrays, *(sums if isinstance(sums, list) else [sums])]
    distinct = []
    for array in inputs:
        if all(array is not other for other in distinct):
            distinct.append(array)
    place = {id(array): at for at, array in enumerate(distinct)}
    sizes = [group[0][0].shape[0] for group in groups]
    total = sum(sizes)
    padded = max(total, LANES)

    def squares_of(refs, low, size):
        height = refs[0].shape[0]
        parts = []
        for start in range(low, low + size, height):
            spare = sum(ref[:, 2 * depth :].astype(jnp.float32) for ref in refs)
            at = start // height * 2 * TERMS
            parts.append(
                [
                    sum(spare[:, first + t : first + t + 1] for t in range(TERMS))
                    for first in (at, at + TERMS)
                ]
            )
        return [jnp.concatenate(column, axis=0) for column in zip(*parts, strict=True)]

    def body(*refs):
        sources = refs[: len(distinct)]
        hgain_ref, egain_ref, wh_ref, we_ref, *outs, normed = refs[len(distinct) :]
        at = 0
        for (arrays, sums, low), size, is_packed in zip(groups, sizes, packed, strict=True):
            arrays = [sources[place[id(array)]] for array in arrays]
            if is_packed:
                squares = squares_of([sources[place[id(array)]] for array in sums], low, size)
            else:
                known = sources[place[id(sums)]]
                squares = [known[low : low + size, column : column + 1] for column in range(2)]
            for column, gain_ref in enumerate((hgain_ref, egain_ref)):
                part = pl.ds(column * depth, depth)
                value = arrays[0][:, part].astype(jnp.float32)
                for other in arrays[1:]:
                    value = value + other[:, part].astype(jnp.float32)
                normed[at : at + size, part] = (
                    value * inverse_rms(squares[column], D) * gain_ref[...]
                ).astype(jnp.bfloat16)
            at += size
        result = (
            jnp.dot(normed[:, :depth], wh_ref[...], preferred_element_type=jnp.float32)
            + jnp.dot(normed[:, depth:], we_ref[...], preferred_element_type=jnp.float32)
        ).astype(jnp.bfloat16)
        if own_first is not None:
            first = result[: total // 2, :]
            second = result[total // 2 : total, :]
            keep = own_first()
            outs[0][...] = jnp.where(keep, first, second)
            outs[1][...] = jnp.where(keep, second, first)
        else:
            outs[0][...] = result[:total, :]

    outputs = [((total, width), jnp.bfloat16)]
    if own_first is not None:
        outputs = [((total // 2, width), jnp.bfloat16)] * 2
    result = kernel(
        body,
        "project",
        [*distinct, hidden_gain, embed_gain, resident(w_hidden), resident(w_embed)],
        outputs,
        [pltpu.VMEM((padded, 2 * depth), jnp.bfloat16)],
        cost,
    )
    return result if own_first is not None else result[0]


def latent_partial(own, received, gain, w_latent, cuts, known=(), route=()):
    rows, width = own.shape
    lat = w_latent.shape[0]
    padded = -(-(lat + 2) // LANES) * LANES
    edge = padded - LANES

    def body(own_ref, received_ref, gain_ref, w_ref, *refs):
        known_refs, mtp_ref, lat_refs = refs[: len(known)], refs[len(known)], refs[len(known) + 1 :]
        mtp = (own_ref[...].astype(jnp.float32) + received_ref[...].astype(jnp.float32)).astype(
            jnp.bfloat16
        )
        mtp_ref[...] = mtp
        wide = mtp.astype(jnp.float32)
        total = jnp.sum(wide * wide, axis=1, keepdims=True)
        normed = (wide * gain_ref[...]).astype(jnp.bfloat16)
        over = (((1,), (1,)), ((), ()))
        main = lax.dot_general(
            normed, w_ref[:edge, :], over, preferred_element_type=jnp.float32
        ).astype(jnp.bfloat16)
        last = lax.dot_general(normed, w_ref[edge:, :], over, preferred_element_type=jnp.float32)
        column = lax.broadcasted_iota(jnp.int32, (rows, padded - lat), 1)
        high_half = total.astype(jnp.bfloat16).astype(jnp.float32)
        spare = jnp.where(column == 0, high_half, jnp.where(column == 1, total - high_half, 0.0))
        last = jnp.concatenate([last, spare], axis=1).astype(jnp.bfloat16)

        def put(ref, part):
            if part < len(known):
                ref[...] = known_refs[part][...]
            else:
                low, high = cuts[part - len(known)]
                ref[:, :edge] = main[low:high, :]
                ref[:, edge:] = last[low:high, :]

        if not route:
            for part, ref in enumerate(lat_refs):
                put(ref, part)
        else:
            lat_refs[0][...] = jnp.zeros_like(lat_refs[0])
            for when, ref in zip(route, lat_refs, strict=True):
                for part in range(len(known) + len(cuts)):
                    pl.when(when(part))(lambda ref=ref, part=part: put(ref, part))

    sizes = [high - low for low, high in cuts]
    outputs = [((rows, width), jnp.bfloat16)]
    outputs += [((size, padded), jnp.bfloat16) for size in ([sizes[0]] * len(route) if route else sizes)]
    mtp, *parts = kernel(body, "latent_partial", [own, received, gain, resident(w_latent), *known], outputs)
    return mtp, parts


def add_early(choices, arrays, rows):
    shape = (rows, choices[0][1].shape[1])

    def body(*refs):
        total = refs[-1]
        value = jnp.zeros(shape, jnp.float32)
        for (when, _), ref in zip(choices, refs, strict=False):
            part = ref[...].astype(jnp.float32)
            value = value + (part if when is None else jnp.where(when(), part, 0.0))
        total[...] = value
        for (at, array), ref in zip(arrays, refs[len(choices) : -1], strict=True):
            total[at : at + array.shape[0], :] += ref[...].astype(jnp.float32)

    inputs = [array for _, array in choices] + [array for _, array in arrays]
    return kernel(body, "add_early", inputs, [(shape, jnp.float32)])[0]


def place_rows(choices, blocks, shape):
    height = shape[0] // blocks

    def body(*refs):
        out = refs[-1]
        for (block, row, when, array), ref in zip(choices, refs, strict=False):

            @pl.when(when())
            def _(block=block, row=row, array=array, ref=ref):
                out[block * height + row : block * height + row + array.shape[0], :] = ref[...]

    return kernel(body, "place_rows", [choice[-1] for choice in choices], [(shape, jnp.bfloat16)])[0]


def finish(base, late, q_gain, kv_gain, cosine, sine_grid, first_row):
    rows = base.shape[0]
    lat = Q_LAT + KV_LAT
    rope = 2 * cosine.shape[1]

    def body(base_ref, *refs):
        late_refs = refs[: len(late)]
        qg_ref, kg_ref, cos_ref, sin_ref, q_ref, kv_ref, rope_ref, total = refs[len(late) :]
        total[...] = base_ref[...]
        for (at, array), ref in zip(late, late_refs, strict=True):
            total[at : at + array.shape[0], :] += ref[...].astype(jnp.float32)
        whole = total[...]
        squares = whole[:, lat + rope : lat + rope + 1] + whole[:, lat + rope + 1 : lat + rope + 2]
        latent = whole * inverse_rms(squares, D)
        q = latent[:, :Q_LAT]
        kv = latent[:, Q_LAT:lat]
        q_scale = inverse_rms(jnp.sum(q * q, axis=1, keepdims=True), Q_LAT)
        kv_scale = inverse_rms(jnp.sum(kv * kv, axis=1, keepdims=True), KV_LAT)
        q_ref[...] = (q * q_scale * qg_ref[...]).astype(jnp.bfloat16)
        kv_ref[...] = (kv * kv_scale * kg_ref[...]).astype(jnp.bfloat16)
        own = pl.ds(pl.multiple_of(first_row(), rows), rows)
        keys = rotate_keys(latent[:, lat : lat + rope], cos_ref[own, :], sin_ref[own, :])
        rope_ref[...] = keys.astype(jnp.bfloat16)

    return kernel(
        body,
        "finish",
        [base, *[array for _, array in late], q_gain, kv_gain, cosine, sine_grid],
        [((rows, Q_LAT), jnp.bfloat16), ((rows, KV_LAT), jnp.bfloat16), ((rows, rope), jnp.bfloat16)],
        [pltpu.VMEM(base.shape, jnp.float32)],
    )


def rounds_of(pairs):
    lists = []
    for source, target in pairs:
        for chosen in lists:
            if all(source != s and target != t for s, t in chosen):
                chosen.append((source, target))
                break
        else:
            lists.append([(source, target)])
    return lists


def shards_line(
    hidden_in, embed_in, hidden_gain, embed_gain, w_hidden, w_embed, attn_gain, w_latent, q_gain, kv_gain
):
    line = lax.axis_size("dp")
    last = line - 1
    shard = hidden_in.shape[0]
    rows_out = shard // 2
    cuts = cuts_of(shard)
    halves = ((0, rows_out), (rows_out, shard))

    def me():
        return lax.axis_index("dp")

    def mine():
        return lax.axis_index("mp")

    def owner(s):
        return s // 2

    def device(d, m):
        return d * 2 + m

    def to_owner(value, senders):
        pairs = [(device(d, 1 - m), device(d, m)) for d, m in senders]
        return lax.ppermute(value, ("dp", "mp"), pairs)

    def shard_of(k, d):
        return sorted({s for s in (d - k, d + k) if 0 <= s < line})

    def senders_of(k):
        return [(d, owner(s)) for d in range(line) for s in shard_of(k, d)]

    def send_latent(k, low, value):
        pairs = []
        for d in range(line):
            for s in shard_of(k, d):
                target = (s % 2) * 2 + low // rows_out
                if target != d:
                    pairs.append((device(d, owner(s)), device(target, owner(s))))
        return [
            (low % rows_out, lax.ppermute(value, ("dp", "mp"), chosen)) for chosen in rounds_of(pairs)
        ]

    pieces, sums = enter(hidden_in, embed_in, cuts)
    tokens = lax.axis_size("mp") * line * rows_out
    tables = rope_tables(
        w_latent.shape[1] - Q_LAT - KV_LAT, jnp.arange(tokens, dtype=jnp.int32) % LENGTH
    )
    small = [gain[None, :] for gain in (hidden_gain, embed_gain, attn_gain, q_gain, kv_gain)] + list(tables)
    (w_hidden, w_embed, w_latent), small = lax.optimization_barrier(((w_hidden, w_embed, w_latent.T), small))
    hidden_gain, embed_gain, attn_gain, q_gain, kv_gain, cosine, sine_grid = small
    weights = (hidden_gain, embed_gain, w_hidden, w_embed)

    other_sums = lax.ppermute(sums, "mp", [(0, 1), (1, 0)])
    piece, sums = pack(hidden_in, embed_in, sums, other_sums, cuts[-1][0])
    pieces.append(piece)
    ahead = [pieces]
    back = [pieces]
    for k in range(1, line):
        if k == 2:
            ahead[1][0], back[1][0], sums = lax.optimization_barrier((ahead[1][0], back[1][0], sums))
            groups = [([piece], sums, low) for piece, (low, _) in zip(pieces, cuts, strict=True)]
            got_own = project(groups, weights, cost=SOME_COST)
            ahead[1][-1], back[1][-1], got_own, sums = lax.optimization_barrier(
                (ahead[1][-1], back[1][-1], got_own, sums)
            )
        ahead.append([lax.ppermute(x, "dp", [(i, i + 1) for i in range(k - 1, last)]) for x in ahead[-1]])
        back.append([lax.ppermute(x, "dp", [(i + 1, i) for i in range(0, line - k)]) for x in back[-1]])
    mtp_own, lat_own = latent_partial(got_own, to_owner(got_own, senders_of(0)), attn_gain, w_latent, halves)
    sums_three = lax.ppermute(sums, "dp", [(0, last), (last, 0)])

    def ahead_is_own():
        near = jnp.where(me() >= 1, me() - 1, me() + 1)
        owned = jnp.where(near >= line // 2, 1, 0) == mine()
        return jnp.where(me() >= 1, owned, jnp.logical_not(owned))

    def routed(offset):
        def when(part):
            to = me() + offset
            to = jnp.where(to >= line, to - line, to)
            upper = jnp.where(to >= line // 2, 1, 0)
            step = jnp.abs(me() - (2 * mine() + upper))
            return jnp.logical_and(step == part // 2, to - upper * (line // 2) == part % 2)

        return when

    one = lax.optimization_barrier((ahead[1], back[1], ahead[2], back[2], lat_own))
    groups = [([x], [one[0][-1]], low) for x, (low, _) in zip(one[0], cuts, strict=True)]
    groups += [([x], [one[1][-1]], low) for x, (low, _) in zip(one[1], cuts, strict=True)]
    got, other = project(groups, weights, own_first=ahead_is_own)
    mtp_one, (lat_base, *lat_routed) = latent_partial(
        got,
        to_owner(other, senders_of(1)),
        attn_gain,
        w_latent,
        halves,
        known=one[4],
        route=[routed(offset) for offset in range(line)],
    )
    early = []
    for offset, part in enumerate(lat_routed, 1):
        pairs = []
        for m in range(2):
            for d in range(line):
                to = (d + offset) % line
                if abs(d - (2 * m + to // 2)) <= 1:
                    pairs.append((device(d, m), device(to, m)))
        early.append((0, lax.ppermute(part, ("dp", "mp"), pairs)))

    two = lax.optimization_barrier((ahead[2], back[2], got))
    groups = [([x, y], [two[0][-1], two[1][-1]], low) for x, y, (low, _) in zip(*two[:2], cuts, strict=True)]
    got = project(groups, weights)
    mtp_two, lat_two = latent_partial(got, to_owner(got, senders_of(2)), attn_gain, w_latent, halves)
    early_two = []
    for (low, _), part in zip(halves, lat_two, strict=True):
        early_two += send_latent(2, low, part)

    mtp_three = []
    late = []
    sums_three = after(sums_three, got, lat_base)
    for x, y, (low, high) in zip(ahead[3], back[3], cuts, strict=True):
        ends = high == shard
        got = project([([x, y], sums_three, low)], weights, cost=MORE_COST if ends else SOME_COST)
        received = to_owner(got, senders_of(3))
        if ends:
            received = after(received, early, early_two)
        mtp, (lat,) = latent_partial(got, received, attn_gain, w_latent, ((0, high - low),))
        mtp_three.append(mtp)
        late += send_latent(3, low, lat)
        sums_three = after(sums_three, got, lat_two)
    early += early_two

    def distance(offset):
        return jnp.abs(me() - (2 * mine() + offset))

    choices = []
    for offset in range(2):
        for k, mtp in enumerate((mtp_own, mtp_one, mtp_two)):
            choices.append((offset, 0, lambda offset=offset, k=k: distance(offset) == k, mtp))
        for (low, _), mtp in zip(cuts, mtp_three, strict=True):
            choices.append((offset, low, lambda offset=offset: distance(offset) == last, mtp))
    mtp_hidden = place_rows(choices, 2, (2 * shard, w_hidden.shape[1]))

    choices = [(None, lat_base)]
    for half, part in enumerate(lat_two):
        choices.append((lambda half=half: routed(0)(2 * 2 + half), part))
    base = add_early(choices, early, rows_out)
    q_latent, kv_latent, key_rope = finish(
        base, late, q_gain, kv_gain, cosine, sine_grid, lambda: (mine() * line + me()) * rows_out
    )
    return (mtp_hidden, q_latent, kv_latent, key_rope)


def cuts_of(shard):
    return ((0, shard // 2), (shard // 2, shard))


def shards_any(
    hidden_in, embed_in, hidden_gain, embed_gain, w_hidden, w_embed, attn_gain, w_latent, q_gain, kv_gain
):
    hidden_wide = hidden_in.astype(jnp.float32)
    embed_wide = embed_in.astype(jnp.float32)
    entry_sums = lax.psum(
        (jnp.sum(hidden_wide * hidden_wide, axis=1), jnp.sum(embed_wide * embed_wide, axis=1)), "mp"
    )
    hidden_norm = (hidden_wide * inverse_rms(entry_sums[0], D)[:, None] * hidden_gain[None, :]).astype(jnp.bfloat16)
    embed_norm = (embed_wide * inverse_rms(entry_sums[1], D)[:, None] * embed_gain[None, :]).astype(jnp.bfloat16)
    hidden_all = lax.all_gather(hidden_norm, "dp", axis=0, tiled=True)
    embed_all = lax.all_gather(embed_norm, "dp", axis=0, tiled=True)
    tok_share = hidden_all.shape[0] // lax.axis_size("mp")
    proj_sum = lax.psum_scatter(
        (
            jnp.dot(hidden_all, w_hidden, preferred_element_type=jnp.float32)
            + jnp.dot(embed_all, w_embed, preferred_element_type=jnp.float32)
        ).astype(jnp.bfloat16),
        "mp",
        scatter_dimension=0,
        tiled=True,
    )
    mtp_hidden = lax.optimization_barrier(proj_sum)
    proj_wide = mtp_hidden.astype(jnp.float32)
    normed_rows = (proj_wide * attn_gain[None, :]).astype(jnp.bfloat16)
    partial_latent = jnp.dot(normed_rows, w_latent, preferred_element_type=jnp.float32)
    rows_out = tok_share // lax.axis_size("dp")
    square_total = lax.psum(jnp.sum(proj_wide * proj_wide, axis=1), "dp")
    latent_sum = lax.psum_scatter(
        partial_latent.astype(jnp.bfloat16), "dp", scatter_dimension=0, tiled=True
    ).astype(jnp.float32)
    first_own = lax.axis_index("dp") * rows_out
    square_sum = lax.dynamic_slice_in_dim(square_total, first_own, rows_out, 0)
    latent = latent_sum * inverse_rms(square_sum, D)[:, None]
    first_token = lax.axis_index("mp") * tok_share + first_own
    positions = (first_token + jnp.arange(rows_out, dtype=jnp.int32)) % LENGTH
    q_latent = latent_norm(latent[:, :Q_LAT], q_gain)
    kv_latent = latent_norm(latent[:, Q_LAT : Q_LAT + KV_LAT], kv_gain)
    rope_part = latent[:, Q_LAT + KV_LAT :]
    key_rope = rotate_keys(rope_part, *rope_tables(rope_part.shape[1], positions)).astype(jnp.bfloat16)
    return (mtp_hidden, q_latent, kv_latent, key_rope)


def solution(mesh):
    placed = (
        P(("branch", "dp"), "mp"),
        P(("branch", "dp"), "mp"),
        P(("branch", "mp")),
        P(("branch", "mp")),
        P(("branch", "mp"), "dp"),
        P(("branch", "mp"), "dp"),
        P(("branch", "dp")),
        P(("branch", "dp"), None),
        P("branch"),
        P("branch"),
    )
    in_line = mesh.shape["dp"] == 4 and mesh.shape["mp"] == 2
    return jax.shard_map(
        shards_line if in_line else shards_any,
        mesh=mesh,
        in_specs=placed,
        out_specs=(
            P(("branch", "mp"), "dp"),
            P(("branch", "mp", "dp"), None),
            P(("branch", "mp", "dp"), None),
            P(("branch", "mp", "dp"), None),
        ),
        check_vma=False,
    )
```

```python
import math

import jax
import jax.numpy as jnp
from jax import lax
from jax.experimental import pallas as pl
from jax.experimental.pallas import tpu as pltpu
from jax.sharding import PartitionSpec as P

D = 7168
Q_LAT = 1536
KV_LAT = 512
LENGTH = 2048
LANES = 128
TERMS = 3
VMEM_BYTES = 9 * 1024 * 1024

epsilon = 1e-06


def inverse_rms(squares_total, width):
    return lax.rsqrt(squares_total / width + epsilon)


def latent_norm(part, gain):
    scale_rows = inverse_rms(jnp.sum(part * part, axis=1), part.shape[1])
    return (part * scale_rows[:, None] * gain[None, :]).astype(jnp.bfloat16)


def rope_tables(width, positions):
    half_width = width // 2
    frequency = jnp.exp(
        jnp.arange(half_width, dtype=jnp.float32) * (-2.0 * math.log(10000.0) / width)
    )
    angle_grid = positions.astype(jnp.float32)[:, None] * frequency[None, :]
    return jnp.cos(angle_grid), jnp.sin(angle_grid)


def rotate_keys(rope_part, cosine, sine_grid):
    half_width = rope_part.shape[1] // 2
    lower_half = rope_part[:, :half_width]
    upper_half = rope_part[:, half_width:]
    return jnp.concatenate(
        [
            lower_half * cosine - upper_half * sine_grid,
            lower_half * sine_grid + upper_half * cosine,
        ],
        axis=1,
    )


def resident(array):
    return pltpu.with_memory_space_constraint(array, pltpu.VMEM)


def after(value, *others):
    return lax.optimization_barrier((value, *others))[0]


VMEM = pl.BlockSpec(memory_space=pltpu.VMEM)
NO_COST = pl.CostEstimate(flops=0, bytes_accessed=0, transcendentals=0)


def kernel(body, name, inputs, outputs, scratch=(), cost=NO_COST):
    return pl.pallas_call(
        body,
        in_specs=[VMEM] * len(inputs),
        out_specs=[VMEM] * len(outputs),
        out_shape=[jax.ShapeDtypeStruct(shape, kind) for shape, kind in outputs],
        scratch_shapes=list(scratch),
        compiler_params=pltpu.CompilerParams(vmem_limit_bytes=VMEM_BYTES),
        cost_estimate=cost,
        name=name,
    )(*inputs)


def half_rows(half, rows, swaps):
    return pl.ds(pl.multiple_of((half + (1 - 2 * half) * swaps) * rows, rows), rows)


def enter(hidden, embed, swaps):
    rows, depth = hidden.shape
    height = rows // 2

    def body(hidden_ref, embed_ref, piece_ref, sums_ref):
        swapped = swaps()
        for half in range(2):
            sums = []
            for column, ref in enumerate((hidden_ref, embed_ref)):
                part = ref[half_rows(half, height, swapped), :]
                if half == 0:
                    piece_ref[:, column * depth : (column + 1) * depth] = part
                wide = part.astype(jnp.float32)
                sums.append(jnp.sum(wide * wide, axis=1, keepdims=True))
            lane = lax.broadcasted_iota(jnp.int32, (height, LANES), 1)
            sums_ref[half * height : (half + 1) * height, :] = jnp.where(
                lane == 0, sums[0], jnp.where(lane == 1, sums[1], 0.0)
            )
        piece_ref[:, 2 * depth :] = jnp.zeros((height, LANES), jnp.bfloat16)

    outputs = [((height, 2 * depth + LANES), jnp.bfloat16), ((rows, LANES), jnp.float32)]
    return kernel(body, "enter", [hidden, embed], outputs)


def pack(hidden, embed, sums, other_sums, swaps):
    rows, depth = hidden.shape
    height = rows // 2

    def body(hidden_ref, embed_ref, sums_ref, other_ref, piece_ref, total_ref):
        total = sums_ref[...] + other_ref[...]
        total_ref[...] = total
        second = half_rows(1, height, swaps())
        piece_ref[:, :depth] = hidden_ref[second, :]
        piece_ref[:, depth : 2 * depth] = embed_ref[second, :]
        lane = lax.broadcasted_iota(jnp.int32, (height, LANES), 1)
        spare = jnp.zeros((height, LANES), jnp.float32)
        at = 0
        for start in range(0, rows, height):
            for column in range(2):
                rest = total[start : start + height, column : column + 1]
                for _ in range(TERMS):
                    term = rest.astype(jnp.bfloat16).astype(jnp.float32)
                    rest = rest - term
                    spare = jnp.where(lane == at, term, spare)
                    at += 1
        piece_ref[:, 2 * depth :] = spare.astype(jnp.bfloat16)

    outputs = [((height, 2 * depth + LANES), jnp.bfloat16), (sums.shape, jnp.float32)]
    return kernel(body, "pack", [hidden, embed, sums, other_sums], outputs)


def project(groups, weights, own_first=None, cost=NO_COST):
    hidden_gain, embed_gain, w_hidden, w_embed = weights
    depth, width = w_hidden.shape
    packed = [isinstance(group[1], list) for group in groups]
    inputs = []
    for arrays, sums, _ in groups:
        inputs += [*arrays, *(sums if isinstance(sums, list) else [sums])]
    distinct = []
    for array in inputs:
        if all(array is not other for other in distinct):
            distinct.append(array)
    place = {id(array): at for at, array in enumerate(distinct)}
    sizes = [group[0][0].shape[0] for group in groups]
    total = sum(sizes)
    padded = max(total, LANES)

    def squares_of(refs, low, size):
        height = refs[0].shape[0]
        parts = []
        for start in range(low, low + size, height):
            spare = sum(ref[:, 2 * depth :].astype(jnp.float32) for ref in refs)
            at = start // height * 2 * TERMS
            parts.append(
                [
                    sum(spare[:, first + t : first + t + 1] for t in range(TERMS))
                    for first in (at, at + TERMS)
                ]
            )
        return [jnp.concatenate(column, axis=0) for column in zip(*parts, strict=True)]

    def body(*refs):
        sources = refs[: len(distinct)]
        hgain_ref, egain_ref, wh_ref, we_ref, *outs, normed = refs[len(distinct) :]
        at = 0
        for (arrays, sums, low), size, is_packed in zip(groups, sizes, packed, strict=True):
            arrays = [sources[place[id(array)]] for array in arrays]
            if is_packed:
                squares = squares_of([sources[place[id(array)]] for array in sums], low, size)
            else:
                known = sources[place[id(sums)]]
                squares = [known[low : low + size, column : column + 1] for column in range(2)]
            for column, gain_ref in enumerate((hgain_ref, egain_ref)):
                part = pl.ds(column * depth, depth)
                value = arrays[0][:, part].astype(jnp.float32)
                for other in arrays[1:]:
                    value = value + other[:, part].astype(jnp.float32)
                normed[at : at + size, part] = (
                    value * inverse_rms(squares[column], D) * gain_ref[...]
                ).astype(jnp.bfloat16)
            at += size
        result = (
            jnp.dot(normed[:, :depth], wh_ref[...], preferred_element_type=jnp.float32)
            + jnp.dot(normed[:, depth:], we_ref[...], preferred_element_type=jnp.float32)
        ).astype(jnp.bfloat16)
        if own_first is not None:
            first = result[: total // 2, :]
            second = result[total // 2 : total, :]
            keep = own_first()
            outs[0][...] = jnp.where(keep, first, second)
            outs[1][...] = jnp.where(keep, second, first)
        else:
            outs[0][...] = result[:total, :]

    outputs = [((total, width), jnp.bfloat16)]
    if own_first is not None:
        outputs = [((total // 2, width), jnp.bfloat16)] * 2
    result = kernel(
        body,
        "project",
        [*distinct, hidden_gain, embed_gain, resident(w_hidden), resident(w_embed)],
        outputs,
        [pltpu.VMEM((padded, 2 * depth), jnp.bfloat16)],
        cost,
    )
    return result if own_first is not None else result[0]


def warm(arrays, weights):
    def body(*refs):
        refs[-1][...] = refs[0][:8, :LANES]

    return kernel(body, "warm", [*arrays, *[resident(w) for w in weights]], [((8, LANES), arrays[0].dtype)])[0]


def choose(first, second, takes_first):
    def body(first_ref, second_ref, out):
        @pl.when(takes_first())
        def _():
            out[...] = first_ref[...]

        @pl.when(jnp.logical_not(takes_first()))
        def _():
            out[...] = second_ref[...]

    return kernel(body, "choose", [first, second], [(first.shape, first.dtype)])[0]


def latent_partial(own, received, gain, w_latent, cuts, known=(), route=()):
    rows, width = own.shape
    lat = w_latent.shape[0]
    padded = -(-(lat + 2) // LANES) * LANES
    edge = padded - LANES

    def body(own_ref, received_ref, gain_ref, w_ref, *refs):
        known_refs, mtp_ref, lat_refs = refs[: len(known)], refs[len(known)], refs[len(known) + 1 :]
        mtp = (own_ref[...].astype(jnp.float32) + received_ref[...].astype(jnp.float32)).astype(
            jnp.bfloat16
        )
        mtp_ref[...] = mtp
        wide = mtp.astype(jnp.float32)
        total = jnp.sum(wide * wide, axis=1, keepdims=True)
        normed = (wide * gain_ref[...]).astype(jnp.bfloat16)
        over = (((1,), (1,)), ((), ()))
        main = lax.dot_general(
            normed, w_ref[:edge, :], over, preferred_element_type=jnp.float32
        ).astype(jnp.bfloat16)
        last = lax.dot_general(normed, w_ref[edge:, :], over, preferred_element_type=jnp.float32)
        column = lax.broadcasted_iota(jnp.int32, (rows, padded - lat), 1)
        high_half = total.astype(jnp.bfloat16).astype(jnp.float32)
        spare = jnp.where(column == 0, high_half, jnp.where(column == 1, total - high_half, 0.0))
        last = jnp.concatenate([last, spare], axis=1).astype(jnp.bfloat16)

        def put(ref, at, part):
            if part < len(known):
                ref[at : at + known[part].shape[0], :] = known_refs[part][...]
            else:
                low, high = cuts[part - len(known)]
                ref[at : at + high - low, :edge] = main[low:high, :]
                ref[at : at + high - low, edge:] = last[low:high, :]

        if not route:
            for part, ref in enumerate(lat_refs):
                put(ref, 0, part)
        for whens, ref in zip(route, lat_refs, strict=False):
            for block, when in enumerate(whens):
                for part in range(len(known) + len(cuts)):
                    pl.when(when() == part)(
                        lambda ref=ref, block=block, part=part: put(ref, block * height, part)
                    )

    sizes = [high - low for low, high in cuts]
    height = sizes[0]
    if route:
        sizes = [height * len(whens) for whens in route]
    outputs = [((rows, width), jnp.bfloat16)] + [((size, padded), jnp.bfloat16) for size in sizes]
    mtp, *parts = kernel(body, "latent_partial", [own, received, gain, resident(w_latent), *known], outputs)
    return mtp, parts


def add_parts(inner, outer, pairs, single, far, is_end):
    rows, width = inner.shape

    def body(inner_ref, outer_ref, first_ref, second_ref, single_ref, far_ref, base_ref, owed_ref):
        outer_sum = outer_ref[...].astype(jnp.float32) + far_ref[...].astype(jnp.float32)
        inner_sum = inner_ref[...].astype(jnp.float32) + single_ref[...].astype(jnp.float32)
        for ref in (first_ref, second_ref):
            inner_sum = inner_sum + ref[:rows, :].astype(jnp.float32)
            outer_sum = outer_sum + ref[rows:, :].astype(jnp.float32)
        base_ref[...] = jnp.where(is_end(), outer_sum, inner_sum)
        owed_ref[...] = outer_sum.astype(jnp.bfloat16)

    return kernel(
        body,
        "add_parts",
        [inner, outer, *pairs, single, far],
        [((rows, width), jnp.float32), ((rows, width), jnp.bfloat16)],
    )


def place_rows(choices, shape, swaps):
    height = shape[0] // 4

    def body(*refs):
        out = refs[-1]
        swapped = swaps()
        for (shard, first, when, array), ref in zip(choices, refs, strict=False):

            @pl.when(when())
            def _(shard=shard, first=first, array=array, ref=ref):
                for at in range(array.shape[0] // height):
                    half = first + at
                    row = (2 * shard + half + (1 - 2 * half) * swapped) * height
                    out[pl.ds(pl.multiple_of(row, height), height), :] = ref[at * height : (at + 1) * height, :]

    return kernel(body, "place_rows", [choice[-1] for choice in choices], [(shape, jnp.bfloat16)])[0]


def finish(base, late, q_gain, kv_gain, cosine, sine_grid, first_row):
    rows = base.shape[0]
    lat = Q_LAT + KV_LAT
    rope = 2 * cosine.shape[1]

    def body(base_ref, *refs):
        late_refs = refs[: len(late)]
        qg_ref, kg_ref, cos_ref, sin_ref, q_ref, kv_ref, rope_ref, total = refs[len(late) :]
        total[...] = base_ref[...]
        for (at, array), ref in zip(late, late_refs, strict=True):
            total[at : at + array.shape[0], :] += ref[...].astype(jnp.float32)
        whole = total[...]
        squares = whole[:, lat + rope : lat + rope + 1] + whole[:, lat + rope + 1 : lat + rope + 2]
        latent = whole * inverse_rms(squares, D)
        q = latent[:, :Q_LAT]
        kv = latent[:, Q_LAT:lat]
        q_scale = inverse_rms(jnp.sum(q * q, axis=1, keepdims=True), Q_LAT)
        kv_scale = inverse_rms(jnp.sum(kv * kv, axis=1, keepdims=True), KV_LAT)
        q_ref[...] = (q * q_scale * qg_ref[...]).astype(jnp.bfloat16)
        kv_ref[...] = (kv * kv_scale * kg_ref[...]).astype(jnp.bfloat16)
        own = pl.ds(pl.multiple_of(first_row(), rows), rows)
        keys = rotate_keys(latent[:, lat : lat + rope], cos_ref[own, :], sin_ref[own, :])
        rope_ref[...] = keys.astype(jnp.bfloat16)

    return kernel(
        body,
        "finish",
        [base, *[array for _, array in late], q_gain, kv_gain, cosine, sine_grid],
        [((rows, Q_LAT), jnp.bfloat16), ((rows, KV_LAT), jnp.bfloat16), ((rows, rope), jnp.bfloat16)],
        [pltpu.VMEM(base.shape, jnp.float32)],
    )


def shards_line(
    hidden_in, embed_in, hidden_gain, embed_gain, w_hidden, w_embed, attn_gain, w_latent, q_gain, kv_gain
):
    line = lax.axis_size("dp")
    last = line - 1
    shard = hidden_in.shape[0]
    rows_out = shard // 2
    halves = ((0, rows_out), (rows_out, shard))

    def me():
        return lax.axis_index("dp")

    def mine():
        return lax.axis_index("mp")

    def owner(s):
        return s // 2

    def device(d, m):
        return d * 2 + m

    def to_owner(value, senders):
        pairs = [(device(d, 1 - m), device(d, m)) for d, m in senders]
        return lax.ppermute(value, ("dp", "mp"), pairs)

    def shard_of(k, d):
        return sorted({s for s in (d - k, d + k) if 0 <= s < line})

    def senders_of(k):
        return [(d, owner(s)) for d in range(line) for s in shard_of(k, d)]

    def upper():
        return jnp.where(me() >= line // 2, 1, 0)

    first_piece, sums = enter(hidden_in, embed_in, upper)
    tokens = lax.axis_size("mp") * line * rows_out
    tables = rope_tables(
        w_latent.shape[1] - Q_LAT - KV_LAT, jnp.arange(tokens, dtype=jnp.int32) % LENGTH
    )
    small = [gain[None, :] for gain in (hidden_gain, embed_gain, attn_gain, q_gain, kv_gain)] + list(tables)
    w_latent = w_latent.T
    hidden_gain, embed_gain, attn_gain, q_gain, kv_gain, cosine, sine_grid = small
    weights = (hidden_gain, embed_gain, w_hidden, w_embed)

    other_sums = lax.ppermute(sums, "mp", [(0, 1), (1, 0)])
    second_piece, sums = pack(hidden_in, embed_in, sums, other_sums, upper)
    pieces = [first_piece, second_piece]
    token = warm([sums, hidden_gain, embed_gain, attn_gain, q_gain, kv_gain, cosine, sine_grid], [w_hidden, w_embed])
    sums_three = lax.ppermute(sums, "dp", [(0, last), (last, 0)])

    def go_ahead(x, k):
        return lax.ppermute(x, "dp", [(i, i + 1) for i in range(k - 1, last)])

    def go_back(x, k):
        return lax.ppermute(x, "dp", [(i + 1, i) for i in range(0, line - k)])

    ahead_one = [go_ahead(x, 1) for x in pieces]
    back_one = [go_back(x, 1) for x in pieces]
    ahead_one[0], back_one[0], token = lax.optimization_barrier((ahead_one[0], back_one[0], token))
    ahead_two = [go_ahead(ahead_one[0], 2)]
    back_two = [go_back(back_one[0], 2)]
    sums = after(sums, token, ahead_one[0], back_one[0])
    groups = [([piece], sums, low) for piece, (low, _) in zip(pieces, halves, strict=True)]
    got_own = project(groups, weights)
    ahead_one[1], back_one[1], got_own, sums_three = lax.optimization_barrier(
        (ahead_one[1], back_one[1], got_own, sums_three)
    )
    ahead_two.append(go_ahead(ahead_one[1], 2))
    back_two.append(go_back(back_one[1], 2))
    mtp_own, lat_own = latent_partial(got_own, to_owner(got_own, senders_of(0)), attn_gain, w_latent, halves)

    def from_ahead():
        return me() >= line // 2

    ahead_two[0], back_two[0], lat_own = lax.optimization_barrier((ahead_two[0], back_two[0], lat_own))
    two = [choose(ahead_two[0], back_two[0], from_ahead)]
    ends_on = [(line - 2, last), (1, 0)]
    three = [lax.ppermute(two[0], "dp", ends_on)]

    def ahead_is_own():
        near = jnp.where(me() >= 1, me() - 1, me() + 1)
        owned = jnp.where(near >= line // 2, 1, 0) == mine()
        return jnp.where(me() >= 1, owned, jnp.logical_not(owned))

    one = lax.optimization_barrier((ahead_one, back_one, two[0]))
    groups = [([x], [one[0][-1]], low) for x, (low, _) in zip(one[0], halves, strict=True)]
    groups += [([x], [one[1][-1]], low) for x, (low, _) in zip(one[1], halves, strict=True)]
    got_one, other_one = project(groups, weights, own_first=ahead_is_own)
    received_one = to_owner(other_one, senders_of(1))
    ahead_two[1], back_two[1], received_one = lax.optimization_barrier(
        (ahead_two[1], back_two[1], received_one)
    )
    two.append(choose(ahead_two[1], back_two[1], from_ahead))
    three.append(lax.ppermute(two[1], "dp", ends_on))
    mtp_one, lat_one = latent_partial(got_one, received_one, attn_gain, w_latent, halves)

    got_two = project([([x], [two[-1]], low) for x, (low, _) in zip(two, halves, strict=True)], weights)
    received_two = to_owner(got_two, senders_of(2))
    sums_three = after(sums_three, got_two)
    got_three = [project([([three[0]], sums_three, 0)], weights)]
    received_two = after(received_two, got_three[0])

    def part_for(half, place):
        return 2 * jnp.abs(me() - (2 * mine() + half)) + jnp.where(mine() == 1, 1 - place, place)

    mtp_two, (inner, outer, away) = latent_partial(
        got_two,
        received_two,
        attn_gain,
        w_latent,
        halves,
        known=[*lat_own, *lat_one],
        route=[
            [lambda: part_for(upper(), 1 - upper())],
            [lambda: part_for(upper(), upper())],
            [lambda: part_for(1 - upper(), upper()), lambda: part_for(1 - upper(), 1 - upper())],
        ],
    )

    def send(value, pairs):
        pairs = [(device(d, m), device(to, m)) for m, d, to in pairs]
        return lax.ppermute(value, ("dp", "mp"), pairs)

    both = range(2)
    crossing = [
        send(away, [(0, 0, 2), (1, 3, 1)]),
        send(away, [(m, d, to) for m in both for d, to in ((1, 2), (2, 1))]),
    ]
    single = send(inner, [(m, d, to) for m in both for d, to in ((0, 1), (3, 2))])

    to_middle = [(0, last, 1), (1, 0, 2)]
    whole = ((0, rows_out),)
    mtp, (lat,) = latent_partial(
        got_three[0], to_owner(got_three[0], senders_of(3)), attn_gain, w_latent, whole
    )
    mtp_three = [mtp]
    far = send(lat, to_middle)
    sums_three = after(sums_three, got_three[0], inner, lat)
    got_three.append(project([([three[1]], sums_three, rows_out)], weights))
    mtp, (lat,) = latent_partial(
        got_three[1], to_owner(got_three[1], senders_of(3)), attn_gain, w_latent, whole
    )
    mtp_three.append(mtp)

    def is_end():
        return jnp.logical_or(me() == 0, me() == last)

    base, owed = add_parts(inner, outer, crossing, single, far, is_end)
    owed = send(owed, [(m, d, to) for m in both for d, to in ((1, 0), (2, last))])
    late = [(0, owed), (0, send(lat, to_middle))]

    def distance(offset):
        return jnp.abs(me() - (2 * mine() + offset))

    choices = []
    for offset in range(2):
        for k, mtp in enumerate((mtp_own, mtp_one, mtp_two)):
            choices.append((offset, 0, lambda offset=offset, k=k: distance(offset) == k, mtp))
        for half, mtp in enumerate(mtp_three):
            choices.append((offset, half, lambda offset=offset: distance(offset) == last, mtp))
    mtp_hidden = place_rows(choices, (2 * shard, w_hidden.shape[1]), mine)

    q_latent, kv_latent, key_rope = finish(
        base, late, q_gain, kv_gain, cosine, sine_grid, lambda: (mine() * line + me()) * rows_out
    )
    return (mtp_hidden, q_latent, kv_latent, key_rope)


def shards_any(
    hidden_in, embed_in, hidden_gain, embed_gain, w_hidden, w_embed, attn_gain, w_latent, q_gain, kv_gain
):
    hidden_wide = hidden_in.astype(jnp.float32)
    embed_wide = embed_in.astype(jnp.float32)
    entry_sums = lax.psum(
        (jnp.sum(hidden_wide * hidden_wide, axis=1), jnp.sum(embed_wide * embed_wide, axis=1)), "mp"
    )
    hidden_norm = (hidden_wide * inverse_rms(entry_sums[0], D)[:, None] * hidden_gain[None, :]).astype(jnp.bfloat16)
    embed_norm = (embed_wide * inverse_rms(entry_sums[1], D)[:, None] * embed_gain[None, :]).astype(jnp.bfloat16)
    hidden_all = lax.all_gather(hidden_norm, "dp", axis=0, tiled=True)
    embed_all = lax.all_gather(embed_norm, "dp", axis=0, tiled=True)
    tok_share = hidden_all.shape[0] // lax.axis_size("mp")
    proj_sum = lax.psum_scatter(
        (
            jnp.dot(hidden_all, w_hidden, preferred_element_type=jnp.float32)
            + jnp.dot(embed_all, w_embed, preferred_element_type=jnp.float32)
        ).astype(jnp.bfloat16),
        "mp",
        scatter_dimension=0,
        tiled=True,
    )
    mtp_hidden = lax.optimization_barrier(proj_sum)
    proj_wide = mtp_hidden.astype(jnp.float32)
    normed_rows = (proj_wide * attn_gain[None, :]).astype(jnp.bfloat16)
    partial_latent = jnp.dot(normed_rows, w_latent, preferred_element_type=jnp.float32)
    rows_out = tok_share // lax.axis_size("dp")
    square_total = lax.psum(jnp.sum(proj_wide * proj_wide, axis=1), "dp")
    latent_sum = lax.psum_scatter(
        partial_latent.astype(jnp.bfloat16), "dp", scatter_dimension=0, tiled=True
    ).astype(jnp.float32)
    first_own = lax.axis_index("dp") * rows_out
    square_sum = lax.dynamic_slice_in_dim(square_total, first_own, rows_out, 0)
    latent = latent_sum * inverse_rms(square_sum, D)[:, None]
    first_token = lax.axis_index("mp") * tok_share + first_own
    positions = (first_token + jnp.arange(rows_out, dtype=jnp.int32)) % LENGTH
    q_latent = latent_norm(latent[:, :Q_LAT], q_gain)
    kv_latent = latent_norm(latent[:, Q_LAT : Q_LAT + KV_LAT], kv_gain)
    rope_part = latent[:, Q_LAT + KV_LAT :]
    key_rope = rotate_keys(rope_part, *rope_tables(rope_part.shape[1], positions)).astype(jnp.bfloat16)
    return (mtp_hidden, q_latent, kv_latent, key_rope)


def solution(mesh):
    placed = (
        P(("branch", "dp"), "mp"),
        P(("branch", "dp"), "mp"),
        P(("branch", "mp")),
        P(("branch", "mp")),
        P(("branch", "mp"), "dp"),
        P(("branch", "mp"), "dp"),
        P(("branch", "dp")),
        P(("branch", "dp"), None),
        P("branch"),
        P("branch"),
    )
    in_line = mesh.shape["dp"] == 4 and mesh.shape["mp"] == 2
    return jax.shard_map(
        shards_line if in_line else shards_any,
        mesh=mesh,
        in_specs=placed,
        out_specs=(
            P(("branch", "mp"), "dp"),
            P(("branch", "mp", "dp"), None),
            P(("branch", "mp", "dp"), None),
            P(("branch", "mp", "dp"), None),
        ),
        check_vma=False,
    )
```

```python
import math

import jax
import jax.numpy as jnp
from jax import lax
from jax.experimental import pallas as pl
from jax.experimental.pallas import tpu as pltpu
from jax.sharding import PartitionSpec as P

D = 7168
Q_LAT = 1536
KV_LAT = 512
LENGTH = 2048
LANES = 128
TERMS = 3
VMEM_BYTES = 6 * 1024 * 1024

epsilon = 1e-06


def inverse_rms(squares_total, width):
    return lax.rsqrt(squares_total / width + epsilon)


def latent_norm(part, gain):
    scale_rows = inverse_rms(jnp.sum(part * part, axis=1), part.shape[1])
    return (part * scale_rows[:, None] * gain[None, :]).astype(jnp.bfloat16)


def rope_tables(width, positions):
    half_width = width // 2
    frequency = jnp.exp(
        jnp.arange(half_width, dtype=jnp.float32) * (-2.0 * math.log(10000.0) / width)
    )
    angle_grid = positions.astype(jnp.float32)[:, None] * frequency[None, :]
    return jnp.cos(angle_grid), jnp.sin(angle_grid)


def rotate_keys(rope_part, cosine, sine_grid):
    half_width = rope_part.shape[1] // 2
    lower_half = rope_part[:, :half_width]
    upper_half = rope_part[:, half_width:]
    return jnp.concatenate(
        [
            lower_half * cosine - upper_half * sine_grid,
            lower_half * sine_grid + upper_half * cosine,
        ],
        axis=1,
    )


def resident(array):
    return pltpu.with_memory_space_constraint(array, pltpu.VMEM)


def after(value, *others):
    return lax.optimization_barrier((value, *others))[0]


VMEM = pl.BlockSpec(memory_space=pltpu.VMEM)
NO_COST = pl.CostEstimate(flops=0, bytes_accessed=0, transcendentals=0)


def kernel(body, name, inputs, outputs, scratch=()):
    return pl.pallas_call(
        body,
        in_specs=[VMEM] * len(inputs),
        out_specs=[VMEM] * len(outputs),
        out_shape=[jax.ShapeDtypeStruct(shape, kind) for shape, kind in outputs],
        scratch_shapes=list(scratch),
        compiler_params=pltpu.CompilerParams(vmem_limit_bytes=VMEM_BYTES),
        cost_estimate=NO_COST,
        name=name,
    )(*inputs)


def half_rows(half, rows, swaps):
    return pl.ds(pl.multiple_of((half + (1 - 2 * half) * swaps) * rows, rows), rows)


def enter(hidden, embed, swaps):
    rows, depth = hidden.shape
    height = rows // 2

    def body(hidden_ref, embed_ref, piece_ref, sums_ref):
        swapped = swaps()
        for half in range(2):
            sums = []
            for column, ref in enumerate((hidden_ref, embed_ref)):
                part = ref[half_rows(half, height, swapped), :]
                if half == 0:
                    piece_ref[:, column * depth : (column + 1) * depth] = part
                wide = part.astype(jnp.float32)
                sums.append(jnp.sum(wide * wide, axis=1, keepdims=True))
            lane = lax.broadcasted_iota(jnp.int32, (height, LANES), 1)
            sums_ref[half * height : (half + 1) * height, :] = jnp.where(
                lane == 0, sums[0], jnp.where(lane == 1, sums[1], 0.0)
            )
        piece_ref[:, 2 * depth :] = jnp.zeros((height, LANES), jnp.bfloat16)

    outputs = [((height, 2 * depth + LANES), jnp.bfloat16), ((rows, LANES), jnp.float32)]
    return kernel(body, "enter", [hidden, embed], outputs)


def pack(hidden, embed, sums, other_sums, swaps):
    rows, depth = hidden.shape
    height = rows // 2

    def body(hidden_ref, embed_ref, sums_ref, other_ref, piece_ref, total_ref):
        total = sums_ref[...] + other_ref[...]
        total_ref[...] = total
        second = half_rows(1, height, swaps())
        piece_ref[:, :depth] = hidden_ref[second, :]
        piece_ref[:, depth : 2 * depth] = embed_ref[second, :]
        lane = lax.broadcasted_iota(jnp.int32, (height, LANES), 1)
        spare = jnp.zeros((height, LANES), jnp.float32)
        at = 0
        for start in range(0, rows, height):
            for column in range(2):
                rest = total[start : start + height, column : column + 1]
                for _ in range(TERMS):
                    term = rest.astype(jnp.bfloat16).astype(jnp.float32)
                    rest = rest - term
                    spare = jnp.where(lane == at, term, spare)
                    at += 1
        piece_ref[:, 2 * depth :] = spare.astype(jnp.bfloat16)

    outputs = [((height, 2 * depth + LANES), jnp.bfloat16), (sums.shape, jnp.float32)]
    return kernel(body, "pack", [hidden, embed, sums, other_sums], outputs)


def project(groups, weights, other_groups=None, takes_first=None, keeps_first=None, needed=None):
    hidden_gain, embed_gain, w_hidden, w_embed = weights
    depth, width = w_hidden.shape
    variants = [groups] if other_groups is None else [groups, other_groups]
    distinct = []
    for variant in variants:
        for array, sums, _ in variant:
            for value in (array, sums):
                if all(value is not other for other in distinct):
                    distinct.append(value)
    place = {id(array): at for at, array in enumerate(distinct)}
    total = sum(group[0].shape[0] for group in groups)
    padded = max(total, LANES)

    def squares_of(ref, low, size):
        if ref.dtype == jnp.float32:
            return [ref[low : low + size, column : column + 1] for column in range(2)]
        spare = ref[:, 2 * depth :].astype(jnp.float32)
        at = low // size * 2 * TERMS
        return [
            sum(spare[:, first + t : first + t + 1] for t in range(TERMS)) for first in (at, at + TERMS)
        ]

    def body(*refs):
        sources = refs[: len(distinct)]
        hgain_ref, egain_ref, wh_ref, we_ref, *outs, normed = refs[len(distinct) :]

        def norm(variant):
            at = 0
            for array, sums, low in variant:
                size = array.shape[0]
                squares = squares_of(sources[place[id(sums)]], low, size)
                for column, gain_ref in enumerate((hgain_ref, egain_ref)):
                    part = pl.ds(column * depth, depth)
                    value = sources[place[id(array)]][:, part].astype(jnp.float32)
                    normed[at : at + size, part] = (
                        value * inverse_rms(squares[column], D) * gain_ref[...]
                    ).astype(jnp.bfloat16)
                at += size

        def run():
            if other_groups is None:
                norm(groups)
            else:
                pl.when(takes_first())(lambda: norm(groups))
                pl.when(jnp.logical_not(takes_first()))(lambda: norm(other_groups))
            result = jnp.dot(normed[:, :depth], wh_ref[...], preferred_element_type=jnp.float32)
            result = result + jnp.dot(normed[:, depth:], we_ref[...], preferred_element_type=jnp.float32)
            result = result[:total, :].astype(jnp.bfloat16)
            if keeps_first is None:
                outs[0][...] = result
            else:
                parts = (result[: total // 2, :], result[total // 2 :, :])
                outs[0][...] = jnp.where(keeps_first(), parts[0], parts[1])
                outs[1][...] = jnp.where(keeps_first(), parts[1], parts[0])

        run() if needed is None else pl.when(needed())(run)

    sizes = [total] if keeps_first is None else [total // 2] * 2
    result = kernel(
        body,
        "project",
        [*distinct, hidden_gain, embed_gain, resident(w_hidden), resident(w_embed)],
        [((size, width), jnp.bfloat16) for size in sizes],
        [pltpu.VMEM((padded, 2 * depth), jnp.bfloat16)],
    )
    return result[0] if keeps_first is None else result


def choose(first, second, takes_first):
    def body(first_ref, second_ref, out):
        @pl.when(takes_first())
        def _():
            out[...] = first_ref[...]

        @pl.when(jnp.logical_not(takes_first()))
        def _():
            out[...] = second_ref[...]

    return kernel(body, "choose", [first, second], [(first.shape, first.dtype)])[0]


def latent_partial(own, received, gain, w_latent, cuts, known=(), route=(), needed=None):
    rows, width = own.shape
    lat = w_latent.shape[0]
    padded = -(-(lat + 2) // LANES) * LANES
    edge = padded - LANES

    def run(own_ref, received_ref, gain_ref, w_ref, *refs):
        known_refs, mtp_ref, lat_refs = refs[: len(known)], refs[len(known)], refs[len(known) + 1 :]
        mtp = (own_ref[...].astype(jnp.float32) + received_ref[...].astype(jnp.float32)).astype(
            jnp.bfloat16
        )
        mtp_ref[...] = mtp
        wide = mtp.astype(jnp.float32)
        total = jnp.sum(wide * wide, axis=1, keepdims=True)
        normed = (wide * gain_ref[...]).astype(jnp.bfloat16)
        over = (((1,), (1,)), ((), ()))
        main = lax.dot_general(
            normed, w_ref[:edge, :], over, preferred_element_type=jnp.float32
        ).astype(jnp.bfloat16)
        last = lax.dot_general(normed, w_ref[edge:, :], over, preferred_element_type=jnp.float32)
        column = lax.broadcasted_iota(jnp.int32, (rows, padded - lat), 1)
        high_half = total.astype(jnp.bfloat16).astype(jnp.float32)
        spare = jnp.where(column == 0, high_half, jnp.where(column == 1, total - high_half, 0.0))
        last = jnp.concatenate([last, spare], axis=1).astype(jnp.bfloat16)

        def put(ref, at, part):
            if part < len(known):
                ref[at : at + known[part].shape[0], :] = known_refs[part][...]
            else:
                low, high = cuts[part - len(known)]
                ref[at : at + high - low, :edge] = main[low:high, :]
                ref[at : at + high - low, edge:] = last[low:high, :]

        if not route:
            for part, ref in enumerate(lat_refs):
                put(ref, 0, part)
        for whens, ref in zip(route, lat_refs, strict=False):
            for block, when in enumerate(whens):
                for part in range(len(known) + len(cuts)):
                    pl.when(when() == part)(
                        lambda ref=ref, block=block, part=part: put(ref, block * height, part)
                    )

    def body(*refs):
        run(*refs) if needed is None else pl.when(needed())(lambda: run(*refs))

    sizes = [high - low for low, high in cuts]
    height = sizes[0]
    if route:
        sizes = [height * len(whens) for whens in route]
    outputs = [((rows, width), jnp.bfloat16)] + [((size, padded), jnp.bfloat16) for size in sizes]
    mtp, *parts = kernel(body, "latent_partial", [own, received, gain, resident(w_latent), *known], outputs)
    return mtp, parts


def add_parts(inner, outer, pairs, single, far, is_end):
    rows, width = inner.shape

    def body(inner_ref, outer_ref, first_ref, second_ref, single_ref, far_ref, base_ref, owed_ref):
        outer_sum = outer_ref[...].astype(jnp.float32) + far_ref[...].astype(jnp.float32)
        inner_sum = inner_ref[...].astype(jnp.float32) + single_ref[...].astype(jnp.float32)
        for ref in (first_ref, second_ref):
            inner_sum = inner_sum + ref[:rows, :].astype(jnp.float32)
            outer_sum = outer_sum + ref[rows:, :].astype(jnp.float32)
        base_ref[...] = jnp.where(is_end(), outer_sum, inner_sum)
        owed_ref[:, :width] = outer_sum.astype(jnp.bfloat16)
        owed_ref[:, width:] = jnp.zeros((rows, LANES), jnp.bfloat16)

    return kernel(
        body,
        "add_parts",
        [inner, outer, *pairs, single, far],
        [((rows, width), jnp.float32), ((rows, width + LANES), jnp.bfloat16)],
    )


def place_rows(choices, shape, swaps):
    height = shape[0] // 4

    def body(*refs):
        *refs, out = refs
        swapped = swaps()
        for shard, first, when, array in choices:
            terms = [refs.pop(0) for _ in (array if isinstance(array, tuple) else (array,))]
            array = array[0] if isinstance(array, tuple) else array

            @pl.when(when())
            def _(shard=shard, first=first, array=array, terms=terms):
                size = min(array.shape[0], height)
                for at in range(array.shape[0] // size):
                    half, within = (first + at, 0) if isinstance(first, int) else (1, first())
                    row = (2 * shard + half + (1 - 2 * half) * swapped) * height + within
                    value = terms[0][at * size : (at + 1) * size, :]
                    if len(terms) > 1:
                        value = value.astype(jnp.float32) + terms[1][...].astype(jnp.float32)
                    out[pl.ds(pl.multiple_of(row, size), size), :] = value.astype(jnp.bfloat16)

    inputs = []
    for choice in choices:
        inputs += choice[-1] if isinstance(choice[-1], tuple) else [choice[-1]]
    return kernel(body, "place_rows", inputs, [(shape, jnp.bfloat16)])[0]


def finish(base, late, q_gain, kv_gain, cosine, sine_grid, first_row):
    rows = base.shape[0]
    lat = Q_LAT + KV_LAT
    rope = 2 * cosine.shape[1]

    def body(base_ref, *refs):
        late_refs = refs[: len(late)]
        qg_ref, kg_ref, cos_ref, sin_ref, q_ref, kv_ref, rope_ref, total = refs[len(late) :]
        total[...] = base_ref[...]
        for (at, array), ref in zip(late, late_refs, strict=True):
            size = array.shape[0]
            total[pl.ds(pl.multiple_of(at(), size), size), :] += ref[:, : total.shape[1]].astype(jnp.float32)
        whole = total[...]
        squares = whole[:, lat + rope : lat + rope + 1] + whole[:, lat + rope + 1 : lat + rope + 2]
        latent = whole * inverse_rms(squares, D)
        q = latent[:, :Q_LAT]
        kv = latent[:, Q_LAT:lat]
        q_scale = inverse_rms(jnp.sum(q * q, axis=1, keepdims=True), Q_LAT)
        kv_scale = inverse_rms(jnp.sum(kv * kv, axis=1, keepdims=True), KV_LAT)
        q_ref[...] = (q * q_scale * qg_ref[...]).astype(jnp.bfloat16)
        kv_ref[...] = (kv * kv_scale * kg_ref[...]).astype(jnp.bfloat16)
        own = pl.ds(pl.multiple_of(first_row(), rows), rows)
        keys = rotate_keys(latent[:, lat : lat + rope], cos_ref[own, :], sin_ref[own, :])
        rope_ref[...] = keys.astype(jnp.bfloat16)

    return kernel(
        body,
        "finish",
        [base, *[array for _, array in late], q_gain, kv_gain, cosine, sine_grid],
        [((rows, Q_LAT), jnp.bfloat16), ((rows, KV_LAT), jnp.bfloat16), ((rows, rope), jnp.bfloat16)],
        [pltpu.VMEM(base.shape, jnp.float32)],
    )


def shards_line(
    hidden_in, embed_in, hidden_gain, embed_gain, w_hidden, w_embed, attn_gain, w_latent, q_gain, kv_gain
):
    line = lax.axis_size("dp")
    last = line - 1
    shard = hidden_in.shape[0]
    rows_out = shard // 2
    halves = ((0, rows_out), (rows_out, shard))

    def me():
        return lax.axis_index("dp")

    def mine():
        return lax.axis_index("mp")

    def owner(s):
        return s // 2

    def device(d, m):
        return d * 2 + m

    def to_owner(value, senders):
        pairs = [(device(d, 1 - m), device(d, m)) for d, m in senders]
        return lax.ppermute(value, ("dp", "mp"), pairs)

    def shard_of(k, d):
        return sorted({s for s in (d - k, d + k) if 0 <= s < line})

    def senders_of(k):
        return [(d, owner(s)) for d in range(line) for s in shard_of(k, d)]

    def upper():
        return jnp.where(me() >= line // 2, 1, 0)

    first_piece, sums = enter(hidden_in, embed_in, upper)
    tokens = lax.axis_size("mp") * line * rows_out
    tables = rope_tables(
        w_latent.shape[1] - Q_LAT - KV_LAT, jnp.arange(tokens, dtype=jnp.int32) % LENGTH
    )
    small = [gain[None, :] for gain in (hidden_gain, embed_gain, attn_gain, q_gain, kv_gain)] + list(tables)
    w_latent = w_latent.T
    hidden_gain, embed_gain, attn_gain, q_gain, kv_gain, cosine, sine_grid = small
    weights = (hidden_gain, embed_gain, w_hidden, w_embed)

    other_sums = lax.ppermute(sums, "mp", [(0, 1), (1, 0)])
    second_piece, sums = pack(hidden_in, embed_in, sums, other_sums, upper)
    pieces = [first_piece, second_piece]
    sums_three = lax.ppermute(sums, "dp", [(0, last), (last, 0)])

    def go_ahead(x, k):
        return lax.ppermute(x, "dp", [(i, i + 1) for i in range(k - 1, last)])

    def go_back(x, k):
        return lax.ppermute(x, "dp", [(i + 1, i) for i in range(0, line - k)])

    ahead_one = [go_ahead(x, 1) for x in pieces]
    back_one = [go_back(x, 1) for x in pieces]
    ahead_two = [go_ahead(ahead_one[0], 2)]
    back_two = [go_back(back_one[0], 2)]
    ahead_one[0], back_one[0], sums = lax.optimization_barrier((ahead_one[0], back_one[0], sums))
    groups = [(piece, sums, low) for piece, (low, _) in zip(pieces, halves, strict=True)]
    got_own = project(groups, weights)
    ahead_one[1], back_one[1], got_own, sums_three = lax.optimization_barrier(
        (ahead_one[1], back_one[1], got_own, sums_three)
    )
    ahead_two.append(go_ahead(ahead_one[1], 2))
    back_two.append(go_back(back_one[1], 2))
    received_own = to_owner(got_own, senders_of(0))
    mtp_own, lat_own = latent_partial(got_own, received_own, attn_gain, w_latent, halves)

    def from_ahead():
        return me() >= line // 2

    def ahead_is_own():
        near = jnp.where(me() >= 1, me() - 1, me() + 1)
        owned = jnp.where(near >= line // 2, 1, 0) == mine()
        return jnp.where(me() >= 1, owned, jnp.logical_not(owned))

    def ahead_is_other():
        return jnp.logical_not(ahead_is_own())

    groups_ahead = [(x, ahead_one[1], low) for x, (low, _) in zip(ahead_one, halves, strict=True)]
    groups_back = [(x, back_one[1], low) for x, (low, _) in zip(back_one, halves, strict=True)]
    received_one = to_owner(project(groups_ahead, weights, groups_back, ahead_is_other), senders_of(1))
    got_one = project(groups_ahead, weights, groups_back, ahead_is_own)
    ahead_two[0], back_two[0], received_one = lax.optimization_barrier(
        (ahead_two[0], back_two[0], received_one)
    )
    two = [choose(ahead_two[0], back_two[0], from_ahead)]
    ends_on = [(line - 2, last), (1, 0)]
    three = [lax.ppermute(two[0], "dp", ends_on)]
    mtp_one, lat_one = latent_partial(got_one, received_one, attn_gain, w_latent, halves)
    ahead_two[1], back_two[1], lat_one, lat_own = lax.optimization_barrier(
        (ahead_two[1], back_two[1], lat_one, lat_own)
    )
    two.append(choose(ahead_two[1], back_two[1], from_ahead))
    three.append(lax.ppermute(two[1], "dp", ends_on))

    def is_end():
        return jnp.logical_or(me() == 0, me() == last)

    got_two = project([(x, two[1], low) for x, (low, _) in zip(two, halves, strict=True)], weights)
    received_two = to_owner(got_two, senders_of(2))
    sums_three = after(sums_three, got_two)
    got_three = [project([(three[0], sums_three, 0)], weights, needed=is_end)]

    def part_for(half, place):
        return 2 * jnp.abs(me() - (2 * mine() + half)) + jnp.where(mine() == 1, 1 - place, place)

    mtp_two, (inner, outer, away) = latent_partial(
        got_two,
        received_two,
        attn_gain,
        w_latent,
        halves,
        known=[*lat_own, *lat_one],
        route=[
            [lambda: part_for(upper(), 1 - upper())],
            [lambda: part_for(upper(), upper())],
            [lambda: part_for(1 - upper(), upper()), lambda: part_for(1 - upper(), 1 - upper())],
        ],
    )

    def send(value, pairs):
        pairs = [(device(d, m), device(to, m)) for m, d, to in pairs]
        return lax.ppermute(value, ("dp", "mp"), pairs)

    both = range(2)
    crossing = [
        send(away, [(0, 0, 2), (1, 3, 1)]),
        send(away, [(m, d, to) for m in both for d, to in ((1, 2), (2, 1))]),
    ]
    single = send(inner, [(m, d, to) for m in both for d, to in ((0, 1), (3, 2))])

    to_middle = [(0, last, 1), (1, 0, 2)]
    whole = ((0, rows_out),)
    mtp, (lat,) = latent_partial(
        got_three[0], to_owner(got_three[0], senders_of(3)), attn_gain, w_latent, whole, needed=is_end
    )
    mtp_three = [mtp]
    far = send(lat, to_middle)
    sums_three = after(sums_three, got_three[0], inner, lat)
    part = rows_out // 2
    kept, given = project([(three[1], sums_three, rows_out)], weights, keeps_first=lambda: mine() == 0, needed=is_end)
    ends = (0, last)
    received = lax.ppermute(
        given, ("dp", "mp"), [(device(d, m), device(d, 1 - m)) for d in ends for m in range(2)]
    )
    mtp, (lat,) = latent_partial(kept, received, attn_gain, w_latent, ((0, part),), needed=is_end)
    mtp_three += [mtp, (given, to_owner(kept, [(last, 0), (0, 1)]))]
    late = [
        (lambda: part * mine(), send(lat, to_middle)),
        (
            lambda: part * (1 - mine()),
            lax.ppermute(lat, ("dp", "mp"), [(device(last, 1), device(1, 0)), (device(0, 0), device(2, 1))]),
        ),
    ]

    base, owed = add_parts(inner, outer, crossing, single, far, is_end)
    owed = send(owed, [(m, d, to) for m in both for d, to in ((1, 0), (2, last))])
    late = [(lambda: 0, owed), *late]

    def distance(offset):
        return jnp.abs(me() - (2 * mine() + offset))

    choices = []
    for offset in range(2):
        for k, mtp in enumerate((mtp_own, mtp_one, mtp_two)):
            choices.append((offset, 0, lambda offset=offset, k=k: distance(offset) == k, mtp))
        for half, mtp in zip((0, lambda: part * mine(), lambda: part * (1 - mine())), mtp_three, strict=True):
            choices.append((offset, half, lambda offset=offset: distance(offset) == last, mtp))
    mtp_hidden = place_rows(choices, (2 * shard, w_hidden.shape[1]), mine)

    q_latent, kv_latent, key_rope = finish(
        base, late, q_gain, kv_gain, cosine, sine_grid, lambda: (mine() * line + me()) * rows_out
    )
    return (mtp_hidden, q_latent, kv_latent, key_rope)


def shards_any(
    hidden_in, embed_in, hidden_gain, embed_gain, w_hidden, w_embed, attn_gain, w_latent, q_gain, kv_gain
):
    hidden_wide = hidden_in.astype(jnp.float32)
    embed_wide = embed_in.astype(jnp.float32)
    entry_sums = lax.psum(
        (jnp.sum(hidden_wide * hidden_wide, axis=1), jnp.sum(embed_wide * embed_wide, axis=1)), "mp"
    )
    hidden_norm = (hidden_wide * inverse_rms(entry_sums[0], D)[:, None] * hidden_gain[None, :]).astype(jnp.bfloat16)
    embed_norm = (embed_wide * inverse_rms(entry_sums[1], D)[:, None] * embed_gain[None, :]).astype(jnp.bfloat16)
    hidden_all = lax.all_gather(hidden_norm, "dp", axis=0, tiled=True)
    embed_all = lax.all_gather(embed_norm, "dp", axis=0, tiled=True)
    tok_share = hidden_all.shape[0] // lax.axis_size("mp")
    proj_sum = lax.psum_scatter(
        (
            jnp.dot(hidden_all, w_hidden, preferred_element_type=jnp.float32)
            + jnp.dot(embed_all, w_embed, preferred_element_type=jnp.float32)
        ).astype(jnp.bfloat16),
        "mp",
        scatter_dimension=0,
        tiled=True,
    )
    mtp_hidden = lax.optimization_barrier(proj_sum)
    proj_wide = mtp_hidden.astype(jnp.float32)
    normed_rows = (proj_wide * attn_gain[None, :]).astype(jnp.bfloat16)
    partial_latent = jnp.dot(normed_rows, w_latent, preferred_element_type=jnp.float32)
    rows_out = tok_share // lax.axis_size("dp")
    square_total = lax.psum(jnp.sum(proj_wide * proj_wide, axis=1), "dp")
    latent_sum = lax.psum_scatter(
        partial_latent.astype(jnp.bfloat16), "dp", scatter_dimension=0, tiled=True
    ).astype(jnp.float32)
    first_own = lax.axis_index("dp") * rows_out
    square_sum = lax.dynamic_slice_in_dim(square_total, first_own, rows_out, 0)
    latent = latent_sum * inverse_rms(square_sum, D)[:, None]
    first_token = lax.axis_index("mp") * tok_share + first_own
    positions = (first_token + jnp.arange(rows_out, dtype=jnp.int32)) % LENGTH
    q_latent = latent_norm(latent[:, :Q_LAT], q_gain)
    kv_latent = latent_norm(latent[:, Q_LAT : Q_LAT + KV_LAT], kv_gain)
    rope_part = latent[:, Q_LAT + KV_LAT :]
    key_rope = rotate_keys(rope_part, *rope_tables(rope_part.shape[1], positions)).astype(jnp.bfloat16)
    return (mtp_hidden, q_latent, kv_latent, key_rope)


def solution(mesh):
    placed = (
        P(("branch", "dp"), "mp"),
        P(("branch", "dp"), "mp"),
        P(("branch", "mp")),
        P(("branch", "mp")),
        P(("branch", "mp"), "dp"),
        P(("branch", "mp"), "dp"),
        P(("branch", "dp")),
        P(("branch", "dp"), None),
        P("branch"),
        P("branch"),
    )
    in_line = mesh.shape["dp"] == 4 and mesh.shape["mp"] == 2
    return jax.shard_map(
        shards_line if in_line else shards_any,
        mesh=mesh,
        in_specs=placed,
        out_specs=(
            P(("branch", "mp"), "dp"),
            P(("branch", "mp", "dp"), None),
            P(("branch", "mp", "dp"), None),
            P(("branch", "mp", "dp"), None),
        ),
        check_vma=False,
    )
```

```python
import math

import jax
import jax.numpy as jnp
from jax import lax
from jax.experimental import pallas as pl
from jax.experimental.pallas import tpu as pltpu
from jax.sharding import PartitionSpec as P

D = 7168
Q_LAT = 1536
KV_LAT = 512
LENGTH = 2048
LANES = 128
TERMS = 3
VMEM_BYTES = 6 * 1024 * 1024
ENTER_BYTES = 56 * 1024 * 1024

epsilon = 1e-06


def inverse_rms(squares_total, width):
    return lax.rsqrt(squares_total / width + epsilon)


def latent_norm(part, gain):
    scale_rows = inverse_rms(jnp.sum(part * part, axis=1), part.shape[1])
    return (part * scale_rows[:, None] * gain[None, :]).astype(jnp.bfloat16)


def rope_tables(width, positions):
    half_width = width // 2
    frequency = jnp.exp(
        jnp.arange(half_width, dtype=jnp.float32) * (-2.0 * math.log(10000.0) / width)
    )
    angle_grid = positions.astype(jnp.float32)[:, None] * frequency[None, :]
    return jnp.cos(angle_grid), jnp.sin(angle_grid)


def rotate_keys(rope_part, cosine, sine_grid):
    half_width = rope_part.shape[1] // 2
    lower_half = rope_part[:, :half_width]
    upper_half = rope_part[:, half_width:]
    return jnp.concatenate(
        [
            lower_half * cosine - upper_half * sine_grid,
            lower_half * sine_grid + upper_half * cosine,
        ],
        axis=1,
    )


def resident(array):
    return pltpu.with_memory_space_constraint(array, pltpu.VMEM)


def after(value, *others):
    return lax.optimization_barrier((value, *others))[0]


VMEM = pl.BlockSpec(memory_space=pltpu.VMEM)
NO_COST = pl.CostEstimate(flops=0, bytes_accessed=0, transcendentals=0)


def kernel(body, name, inputs, outputs, scratch=(), place=VMEM, vmem=VMEM_BYTES):
    return pl.pallas_call(
        body,
        in_specs=[place] * len(inputs),
        out_specs=[VMEM] * len(outputs),
        out_shape=[jax.ShapeDtypeStruct(shape, kind) for shape, kind in outputs],
        scratch_shapes=list(scratch),
        compiler_params=pltpu.CompilerParams(vmem_limit_bytes=vmem),
        cost_estimate=NO_COST,
        name=name,
    )(*inputs)


def half_rows(half, rows, swaps):
    return pl.ds(pl.multiple_of((half + (1 - 2 * half) * swaps) * rows, rows), rows)


def enter(hidden, embed, swaps):
    rows, depth = hidden.shape
    height = rows // 2

    def body(hidden_ref, embed_ref, piece_ref, sems):
        part = half_rows(0, height, swaps())
        copies = [
            pltpu.make_async_copy(
                ref.at[part, :], piece_ref.at[:, pl.ds(column * depth, depth)], sems.at[column]
            )
            for column, ref in enumerate((hidden_ref, embed_ref))
        ]
        for copy in copies:
            copy.start()
        for copy in copies:
            copy.wait()

    return kernel(
        body,
        "enter",
        [hidden, embed],
        [((height, 2 * depth), jnp.bfloat16)],
        [pltpu.SemaphoreType.DMA((2,))],
        place=pl.BlockSpec(memory_space=pl.ANY),
        vmem=ENTER_BYTES,
    )[0]


def add_squares(hidden, embed, swaps):
    rows = hidden.shape[0]
    height = rows // 2

    def body(hidden_ref, embed_ref, sums_ref):
        swapped = swaps()
        lane = lax.broadcasted_iota(jnp.int32, (height, LANES), 1)
        for half in range(2):
            total = jnp.zeros((height, LANES), jnp.float32)
            for column, ref in enumerate((hidden_ref, embed_ref)):
                wide = ref[half_rows(half, height, swapped), :].astype(jnp.float32)
                total = jnp.where(lane == column, jnp.sum(wide * wide, axis=1, keepdims=True), total)
            sums_ref[half * height : (half + 1) * height, :] = total

    return kernel(body, "add_squares", [hidden, embed], [((rows, LANES), jnp.float32)])[0]


def pack(hidden, embed, sums, other_sums, swaps):
    rows, depth = hidden.shape
    height = rows // 2

    def body(hidden_ref, embed_ref, sums_ref, other_ref, piece_ref, total_ref):
        total = sums_ref[...] + other_ref[...]
        total_ref[...] = total
        second = half_rows(1, height, swaps())
        piece_ref[:, :depth] = hidden_ref[second, :]
        piece_ref[:, depth : 2 * depth] = embed_ref[second, :]
        lane = lax.broadcasted_iota(jnp.int32, (height, LANES), 1)
        spare = jnp.zeros((height, LANES), jnp.float32)
        at = 0
        for start in range(0, rows, height):
            for column in range(2):
                rest = total[start : start + height, column : column + 1]
                for _ in range(TERMS):
                    term = rest.astype(jnp.bfloat16).astype(jnp.float32)
                    rest = rest - term
                    spare = jnp.where(lane == at, term, spare)
                    at += 1
        piece_ref[:, 2 * depth :] = spare.astype(jnp.bfloat16)

    outputs = [((height, 2 * depth + LANES), jnp.bfloat16), (sums.shape, jnp.float32)]
    return kernel(body, "pack", [hidden, embed, sums, other_sums], outputs)


def project(groups, weights, other_groups=None, takes_first=None, keeps_first=None, needed=None):
    hidden_gain, embed_gain, w_hidden, w_embed = weights
    depth, width = w_hidden.shape
    variants = [groups] if other_groups is None else [groups, other_groups]
    distinct = []
    for variant in variants:
        for array, sums, _ in variant:
            for value in (array, sums):
                if all(value is not other for other in distinct):
                    distinct.append(value)
    place = {id(array): at for at, array in enumerate(distinct)}
    total = sum(group[0].shape[0] for group in groups)
    padded = max(total, LANES)

    def squares_of(ref, low, size):
        if ref.dtype == jnp.float32:
            return [ref[low : low + size, column : column + 1] for column in range(2)]
        spare = ref[:, 2 * depth :].astype(jnp.float32)
        at = low // size * 2 * TERMS
        return [
            sum(spare[:, first + t : first + t + 1] for t in range(TERMS)) for first in (at, at + TERMS)
        ]

    def body(*refs):
        sources = refs[: len(distinct)]
        hgain_ref, egain_ref, wh_ref, we_ref, *outs, normed = refs[len(distinct) :]

        def norm(variant):
            at = 0
            for array, sums, low in variant:
                size = array.shape[0]
                squares = squares_of(sources[place[id(sums)]], low, size)
                for column, gain_ref in enumerate((hgain_ref, egain_ref)):
                    part = pl.ds(column * depth, depth)
                    value = sources[place[id(array)]][:, part].astype(jnp.float32)
                    normed[at : at + size, part] = (
                        value * inverse_rms(squares[column], D) * gain_ref[...]
                    ).astype(jnp.bfloat16)
                at += size

        def run():
            if other_groups is None:
                norm(groups)
            else:
                pl.when(takes_first())(lambda: norm(groups))
                pl.when(jnp.logical_not(takes_first()))(lambda: norm(other_groups))
            result = jnp.dot(normed[:, :depth], wh_ref[...], preferred_element_type=jnp.float32)
            result = result + jnp.dot(normed[:, depth:], we_ref[...], preferred_element_type=jnp.float32)
            result = result[:total, :].astype(jnp.bfloat16)
            if keeps_first is None:
                outs[0][...] = result
            else:
                parts = (result[: total // 2, :], result[total // 2 :, :])
                outs[0][...] = jnp.where(keeps_first(), parts[0], parts[1])
                outs[1][...] = jnp.where(keeps_first(), parts[1], parts[0])

        run() if needed is None else pl.when(needed())(run)

    sizes = [total] if keeps_first is None else [total // 2] * 2
    result = kernel(
        body,
        "project",
        [*distinct, hidden_gain, embed_gain, resident(w_hidden), resident(w_embed)],
        [((size, width), jnp.bfloat16) for size in sizes],
        [pltpu.VMEM((padded, 2 * depth), jnp.bfloat16)],
    )
    return result[0] if keeps_first is None else result


def latent_partial(own, received, gain, w_latent, cuts, known=(), route=(), needed=None):
    rows, width = own.shape
    lat = w_latent.shape[0]
    padded = -(-(lat + 2) // LANES) * LANES
    edge = padded - LANES

    def run(own_ref, received_ref, gain_ref, w_ref, *refs):
        known_refs, mtp_ref, lat_refs = refs[: len(known)], refs[len(known)], refs[len(known) + 1 :]
        mtp = (own_ref[...].astype(jnp.float32) + received_ref[...].astype(jnp.float32)).astype(
            jnp.bfloat16
        )
        mtp_ref[...] = mtp
        wide = mtp.astype(jnp.float32)
        total = jnp.sum(wide * wide, axis=1, keepdims=True)
        normed = (wide * gain_ref[...]).astype(jnp.bfloat16)
        over = (((1,), (1,)), ((), ()))
        main = lax.dot_general(
            normed, w_ref[:edge, :], over, preferred_element_type=jnp.float32
        ).astype(jnp.bfloat16)
        last = lax.dot_general(normed, w_ref[edge:, :], over, preferred_element_type=jnp.float32)
        column = lax.broadcasted_iota(jnp.int32, (rows, padded - lat), 1)
        high_half = total.astype(jnp.bfloat16).astype(jnp.float32)
        spare = jnp.where(column == 0, high_half, jnp.where(column == 1, total - high_half, 0.0))
        last = jnp.concatenate([last, spare], axis=1).astype(jnp.bfloat16)

        def put(ref, at, part):
            if part < len(known):
                ref[at : at + known[part].shape[0], :] = known_refs[part][...]
            else:
                low, high = cuts[part - len(known)]
                ref[at : at + high - low, :edge] = main[low:high, :]
                ref[at : at + high - low, edge:] = last[low:high, :]

        if not route:
            for part, ref in enumerate(lat_refs):
                put(ref, 0, part)
        for whens, ref in zip(route, lat_refs, strict=False):
            for block, when in enumerate(whens):
                for part in range(len(known) + len(cuts)):
                    pl.when(when() == part)(
                        lambda ref=ref, block=block, part=part: put(ref, block * height, part)
                    )

    def body(*refs):
        run(*refs) if needed is None else pl.when(needed())(lambda: run(*refs))

    sizes = [high - low for low, high in cuts]
    height = sizes[0]
    if route:
        sizes = [height * len(whens) for whens in route]
    outputs = [((rows, width), jnp.bfloat16)] + [((size, padded), jnp.bfloat16) for size in sizes]
    mtp, *parts = kernel(body, "latent_partial", [own, received, gain, resident(w_latent), *known], outputs)
    return mtp, parts


def add_parts(inner, outer, pairs, single, far, is_end):
    rows, width = inner.shape

    def body(inner_ref, outer_ref, first_ref, second_ref, single_ref, far_ref, base_ref, owed_ref):
        outer_sum = outer_ref[...].astype(jnp.float32) + far_ref[...].astype(jnp.float32)
        inner_sum = inner_ref[...].astype(jnp.float32) + single_ref[...].astype(jnp.float32)
        for ref in (first_ref, second_ref):
            inner_sum = inner_sum + ref[:rows, :].astype(jnp.float32)
            outer_sum = outer_sum + ref[rows:, :].astype(jnp.float32)
        base_ref[...] = jnp.where(is_end(), outer_sum, inner_sum)
        owed_ref[:, :width] = outer_sum.astype(jnp.bfloat16)
        owed_ref[:, width:] = jnp.zeros((rows, LANES), jnp.bfloat16)

    return kernel(
        body,
        "add_parts",
        [inner, outer, *pairs, single, far],
        [((rows, width), jnp.float32), ((rows, width + LANES), jnp.bfloat16)],
    )


def place_rows(choices, shape, swaps):
    height = shape[0] // 4

    def body(*refs):
        *refs, out = refs
        swapped = swaps()
        for shard, first, when, array in choices:
            terms = [refs.pop(0) for _ in (array if isinstance(array, tuple) else (array,))]
            array = array[0] if isinstance(array, tuple) else array

            @pl.when(when())
            def _(shard=shard, first=first, array=array, terms=terms):
                size = min(array.shape[0], height)
                for at in range(array.shape[0] // size):
                    half, within = (first + at, 0) if isinstance(first, int) else (1, first())
                    row = (2 * shard + half + (1 - 2 * half) * swapped) * height + within
                    value = terms[0][at * size : (at + 1) * size, :]
                    if len(terms) > 1:
                        value = value.astype(jnp.float32) + terms[1][...].astype(jnp.float32)
                    out[pl.ds(pl.multiple_of(row, size), size), :] = value.astype(jnp.bfloat16)

    inputs = []
    for choice in choices:
        inputs += choice[-1] if isinstance(choice[-1], tuple) else [choice[-1]]
    return kernel(body, "place_rows", inputs, [(shape, jnp.bfloat16)])[0]


def finish(base, late, q_gain, kv_gain, cosine, sine_grid, first_row):
    rows = base.shape[0]
    lat = Q_LAT + KV_LAT
    rope = 2 * cosine.shape[1]

    def body(base_ref, *refs):
        late_refs = refs[: len(late)]
        qg_ref, kg_ref, cos_ref, sin_ref, q_ref, kv_ref, rope_ref, total = refs[len(late) :]
        total[...] = base_ref[...]
        for (at, array), ref in zip(late, late_refs, strict=True):
            size = array.shape[0]
            total[pl.ds(pl.multiple_of(at(), size), size), :] += ref[:, : total.shape[1]].astype(jnp.float32)
        whole = total[...]
        squares = whole[:, lat + rope : lat + rope + 1] + whole[:, lat + rope + 1 : lat + rope + 2]
        latent = whole * inverse_rms(squares, D)
        q = latent[:, :Q_LAT]
        kv = latent[:, Q_LAT:lat]
        q_scale = inverse_rms(jnp.sum(q * q, axis=1, keepdims=True), Q_LAT)
        kv_scale = inverse_rms(jnp.sum(kv * kv, axis=1, keepdims=True), KV_LAT)
        q_ref[...] = (q * q_scale * qg_ref[...]).astype(jnp.bfloat16)
        kv_ref[...] = (kv * kv_scale * kg_ref[...]).astype(jnp.bfloat16)
        own = pl.ds(pl.multiple_of(first_row(), rows), rows)
        keys = rotate_keys(latent[:, lat : lat + rope], cos_ref[own, :], sin_ref[own, :])
        rope_ref[...] = keys.astype(jnp.bfloat16)

    return kernel(
        body,
        "finish",
        [base, *[array for _, array in late], q_gain, kv_gain, cosine, sine_grid],
        [((rows, Q_LAT), jnp.bfloat16), ((rows, KV_LAT), jnp.bfloat16), ((rows, rope), jnp.bfloat16)],
        [pltpu.VMEM(base.shape, jnp.float32)],
    )


def shards_line(
    hidden_in, embed_in, hidden_gain, embed_gain, w_hidden, w_embed, attn_gain, w_latent, q_gain, kv_gain
):
    line = lax.axis_size("dp")
    last = line - 1
    shard = hidden_in.shape[0]
    rows_out = shard // 2
    halves = ((0, rows_out), (rows_out, shard))

    def me():
        return lax.axis_index("dp")

    def mine():
        return lax.axis_index("mp")

    def owner(s):
        return s // 2

    def device(d, m):
        return d * 2 + m

    def to_owner(value, senders):
        pairs = [(device(d, 1 - m), device(d, m)) for d, m in senders]
        return lax.ppermute(value, ("dp", "mp"), pairs)

    def shard_of(k, d):
        return sorted({s for s in (d - k, d + k) if 0 <= s < line})

    def senders_of(k):
        return [(d, owner(s)) for d in range(line) for s in shard_of(k, d)]

    def upper():
        return jnp.where(me() >= line // 2, 1, 0)

    first_piece = enter(hidden_in, embed_in, upper)
    sums = add_squares(hidden_in, embed_in, upper)
    tokens = lax.axis_size("mp") * line * rows_out
    tables = rope_tables(
        w_latent.shape[1] - Q_LAT - KV_LAT, jnp.arange(tokens, dtype=jnp.int32) % LENGTH
    )
    small = [gain[None, :] for gain in (hidden_gain, embed_gain, attn_gain, q_gain, kv_gain)] + list(tables)
    w_latent = w_latent.T
    hidden_gain, embed_gain, attn_gain, q_gain, kv_gain, cosine, sine_grid = small
    weights = (hidden_gain, embed_gain, w_hidden, w_embed)

    other_sums = lax.ppermute(sums, "mp", [(0, 1), (1, 0)])
    second_piece, sums = pack(hidden_in, embed_in, sums, other_sums, upper)
    pieces = [first_piece, second_piece]
    sums_three = lax.ppermute(sums, "dp", [(0, last), (last, 0)])

    pairs_on = [(0, 1), (1, 0), (2, 3), (3, 2)]
    middle_on = [(1, 2), (2, 1)]
    ends_on = [(2, 3), (1, 0)]
    pair_one = [lax.ppermute(x, "dp", pairs_on) for x in pieces]
    cross_one = [lax.ppermute(x, "dp", middle_on) for x in pieces]
    ends_two = [lax.ppermute(cross_one[0], "dp", ends_on)]
    middle_two = [lax.ppermute(pair_one[0], "dp", middle_on)]
    pair_one[0], cross_one[0], sums = lax.optimization_barrier((pair_one[0], cross_one[0], sums))
    groups = [(piece, sums, low) for piece, (low, _) in zip(pieces, halves, strict=True)]
    got_own = project(groups, weights)
    pair_one[1], cross_one[1], got_own, sums_three = lax.optimization_barrier(
        (pair_one[1], cross_one[1], got_own, sums_three)
    )
    ends_two.append(lax.ppermute(cross_one[1], "dp", ends_on))
    middle_two.append(lax.ppermute(pair_one[1], "dp", middle_on))
    received_own = to_owner(got_own, senders_of(0))
    mtp_own, lat_own = latent_partial(got_own, received_own, attn_gain, w_latent, halves)

    def pair_is_own():
        return upper() == mine()

    def pair_is_other():
        return upper() != mine()

    groups_pair = [(x, pair_one[1], low) for x, (low, _) in zip(pair_one, halves, strict=True)]
    groups_cross = [(x, cross_one[1], low) for x, (low, _) in zip(cross_one, halves, strict=True)]
    received_one = to_owner(project(groups_pair, weights, groups_cross, pair_is_other), senders_of(1))
    got_one = project(groups_pair, weights, groups_cross, pair_is_own)
    middle_two[0], ends_two[0], received_one = lax.optimization_barrier(
        (middle_two[0], ends_two[0], received_one)
    )
    three = [lax.ppermute(middle_two[0], "dp", ends_on)]
    mtp_one, lat_one = latent_partial(got_one, received_one, attn_gain, w_latent, halves)
    middle_two[1], ends_two[1], lat_one, lat_own = lax.optimization_barrier(
        (middle_two[1], ends_two[1], lat_one, lat_own)
    )
    three.append(lax.ppermute(middle_two[1], "dp", ends_on))

    def is_end():
        return jnp.logical_or(me() == 0, me() == last)

    groups_ends = [(x, ends_two[1], low) for x, (low, _) in zip(ends_two, halves, strict=True)]
    groups_middle = [(x, middle_two[1], low) for x, (low, _) in zip(middle_two, halves, strict=True)]
    got_two = project(groups_ends, weights, groups_middle, is_end)
    received_two = to_owner(got_two, senders_of(2))
    sums_three = after(sums_three, got_two)
    got_three = [project([(three[0], sums_three, 0)], weights, needed=is_end)]
    received_two = after(received_two, got_three[0])

    def part_for(half, place):
        return 2 * jnp.abs(me() - (2 * mine() + half)) + jnp.where(mine() == 1, 1 - place, place)

    mtp_two, (inner, outer, away) = latent_partial(
        got_two,
        received_two,
        attn_gain,
        w_latent,
        halves,
        known=[*lat_own, *lat_one],
        route=[
            [lambda: part_for(upper(), 1 - upper())],
            [lambda: part_for(upper(), upper())],
            [lambda: part_for(1 - upper(), upper()), lambda: part_for(1 - upper(), 1 - upper())],
        ],
    )

    def send(value, pairs):
        pairs = [(device(d, m), device(to, m)) for m, d, to in pairs]
        return lax.ppermute(value, ("dp", "mp"), pairs)

    both = range(2)
    crossing = [
        send(away, [(0, 0, 2), (1, 3, 1)]),
        send(away, [(m, d, to) for m in both for d, to in ((1, 2), (2, 1))]),
    ]
    single = send(inner, [(m, d, to) for m in both for d, to in ((0, 1), (3, 2))])

    to_middle = [(0, last, 1), (1, 0, 2)]
    whole = ((0, rows_out),)
    mtp, (lat,) = latent_partial(
        got_three[0], to_owner(got_three[0], senders_of(3)), attn_gain, w_latent, whole, needed=is_end
    )
    mtp_three = [mtp]
    far = send(lat, to_middle)
    sums_three = after(sums_three, got_three[0], inner, lat)
    part = rows_out // 2
    kept, given = project([(three[1], sums_three, rows_out)], weights, keeps_first=lambda: mine() == 0, needed=is_end)
    ends = (0, last)
    received = lax.ppermute(
        given, ("dp", "mp"), [(device(d, m), device(d, 1 - m)) for d in ends for m in range(2)]
    )
    mtp, (lat,) = latent_partial(kept, received, attn_gain, w_latent, ((0, part),), needed=is_end)
    mtp_three += [mtp, (given, to_owner(kept, [(last, 0), (0, 1)]))]
    late = [
        (lambda: part * mine(), send(lat, to_middle)),
        (
            lambda: part * (1 - mine()),
            lax.ppermute(lat, ("dp", "mp"), [(device(last, 1), device(1, 0)), (device(0, 0), device(2, 1))]),
        ),
    ]

    base, owed = add_parts(inner, outer, crossing, single, far, is_end)
    owed = send(owed, [(m, d, to) for m in both for d, to in ((1, 0), (2, last))])
    late = [(lambda: 0, owed), *late]

    def distance(offset):
        return jnp.abs(me() - (2 * mine() + offset))

    choices = []
    for offset in range(2):
        for k, mtp in enumerate((mtp_own, mtp_one, mtp_two)):
            choices.append((offset, 0, lambda offset=offset, k=k: distance(offset) == k, mtp))
        for half, mtp in zip((0, lambda: part * mine(), lambda: part * (1 - mine())), mtp_three, strict=True):
            choices.append((offset, half, lambda offset=offset: distance(offset) == last, mtp))
    mtp_hidden = place_rows(choices, (2 * shard, w_hidden.shape[1]), mine)

    q_latent, kv_latent, key_rope = finish(
        base, late, q_gain, kv_gain, cosine, sine_grid, lambda: (mine() * line + me()) * rows_out
    )
    return (mtp_hidden, q_latent, kv_latent, key_rope)


def shards_any(
    hidden_in, embed_in, hidden_gain, embed_gain, w_hidden, w_embed, attn_gain, w_latent, q_gain, kv_gain
):
    hidden_wide = hidden_in.astype(jnp.float32)
    embed_wide = embed_in.astype(jnp.float32)
    entry_sums = lax.psum(
        (jnp.sum(hidden_wide * hidden_wide, axis=1), jnp.sum(embed_wide * embed_wide, axis=1)), "mp"
    )
    hidden_norm = (hidden_wide * inverse_rms(entry_sums[0], D)[:, None] * hidden_gain[None, :]).astype(jnp.bfloat16)
    embed_norm = (embed_wide * inverse_rms(entry_sums[1], D)[:, None] * embed_gain[None, :]).astype(jnp.bfloat16)
    hidden_all = lax.all_gather(hidden_norm, "dp", axis=0, tiled=True)
    embed_all = lax.all_gather(embed_norm, "dp", axis=0, tiled=True)
    tok_share = hidden_all.shape[0] // lax.axis_size("mp")
    proj_sum = lax.psum_scatter(
        (
            jnp.dot(hidden_all, w_hidden, preferred_element_type=jnp.float32)
            + jnp.dot(embed_all, w_embed, preferred_element_type=jnp.float32)
        ).astype(jnp.bfloat16),
        "mp",
        scatter_dimension=0,
        tiled=True,
    )
    mtp_hidden = lax.optimization_barrier(proj_sum)
    proj_wide = mtp_hidden.astype(jnp.float32)
    normed_rows = (proj_wide * attn_gain[None, :]).astype(jnp.bfloat16)
    partial_latent = jnp.dot(normed_rows, w_latent, preferred_element_type=jnp.float32)
    rows_out = tok_share // lax.axis_size("dp")
    square_total = lax.psum(jnp.sum(proj_wide * proj_wide, axis=1), "dp")
    latent_sum = lax.psum_scatter(
        partial_latent.astype(jnp.bfloat16), "dp", scatter_dimension=0, tiled=True
    ).astype(jnp.float32)
    first_own = lax.axis_index("dp") * rows_out
    square_sum = lax.dynamic_slice_in_dim(square_total, first_own, rows_out, 0)
    latent = latent_sum * inverse_rms(square_sum, D)[:, None]
    first_token = lax.axis_index("mp") * tok_share + first_own
    positions = (first_token + jnp.arange(rows_out, dtype=jnp.int32)) % LENGTH
    q_latent = latent_norm(latent[:, :Q_LAT], q_gain)
    kv_latent = latent_norm(latent[:, Q_LAT : Q_LAT + KV_LAT], kv_gain)
    rope_part = latent[:, Q_LAT + KV_LAT :]
    key_rope = rotate_keys(rope_part, *rope_tables(rope_part.shape[1], positions)).astype(jnp.bfloat16)
    return (mtp_hidden, q_latent, kv_latent, key_rope)


def solution(mesh):
    placed = (
        P(("branch", "dp"), "mp"),
        P(("branch", "dp"), "mp"),
        P(("branch", "mp")),
        P(("branch", "mp")),
        P(("branch", "mp"), "dp"),
        P(("branch", "mp"), "dp"),
        P(("branch", "dp")),
        P(("branch", "dp"), None),
        P("branch"),
        P("branch"),
    )
    in_line = mesh.shape["dp"] == 4 and mesh.shape["mp"] == 2
    return jax.shard_map(
        shards_line if in_line else shards_any,
        mesh=mesh,
        in_specs=placed,
        out_specs=(
            P(("branch", "mp"), "dp"),
            P(("branch", "mp", "dp"), None),
            P(("branch", "mp", "dp"), None),
            P(("branch", "mp", "dp"), None),
        ),
        check_vma=False,
    )
```

```python
import math

import jax
import jax.numpy as jnp
from jax import lax
from jax.experimental import pallas as pl
from jax.experimental.pallas import tpu as pltpu
from jax.sharding import PartitionSpec as P

D = 7168
Q_LAT = 1536
KV_LAT = 512
LENGTH = 2048
LANES = 128
TERMS = 3
VMEM_BYTES = 6 * 1024 * 1024
ENTER_BYTES = 56 * 1024 * 1024

epsilon = 1e-06


def inverse_rms(squares_total, width):
    return lax.rsqrt(squares_total / width + epsilon)


def latent_norm(part, gain):
    scale_rows = inverse_rms(jnp.sum(part * part, axis=1), part.shape[1])
    return (part * scale_rows[:, None] * gain[None, :]).astype(jnp.bfloat16)


def rope_tables(width, positions):
    half_width = width // 2
    frequency = jnp.exp(
        jnp.arange(half_width, dtype=jnp.float32) * (-2.0 * math.log(10000.0) / width)
    )
    angle_grid = positions.astype(jnp.float32)[:, None] * frequency[None, :]
    return jnp.cos(angle_grid), jnp.sin(angle_grid)


def rotate_keys(rope_part, cosine, sine_grid):
    half_width = rope_part.shape[1] // 2
    lower_half = rope_part[:, :half_width]
    upper_half = rope_part[:, half_width:]
    return jnp.concatenate(
        [
            lower_half * cosine - upper_half * sine_grid,
            lower_half * sine_grid + upper_half * cosine,
        ],
        axis=1,
    )


def resident(array):
    return pltpu.with_memory_space_constraint(array, pltpu.VMEM)


def after(value, *others):
    return lax.optimization_barrier((value, *others))[0]


VMEM = pl.BlockSpec(memory_space=pltpu.VMEM)
NO_COST = pl.CostEstimate(flops=0, bytes_accessed=0, transcendentals=0)


def kernel(body, name, inputs, outputs, scratch=(), place=VMEM, vmem=VMEM_BYTES):
    return pl.pallas_call(
        body,
        in_specs=[place] * len(inputs),
        out_specs=[VMEM] * len(outputs),
        out_shape=[jax.ShapeDtypeStruct(shape, kind) for shape, kind in outputs],
        scratch_shapes=list(scratch),
        compiler_params=pltpu.CompilerParams(vmem_limit_bytes=vmem),
        cost_estimate=NO_COST,
        name=name,
    )(*inputs)


def half_rows(half, rows, swaps):
    return pl.ds(pl.multiple_of((half + (1 - 2 * half) * swaps) * rows, rows), rows)


def enter(hidden, embed, swaps):
    rows, depth = hidden.shape
    height = rows // 2

    def body(hidden_ref, embed_ref, piece_ref, sems):
        part = half_rows(0, height, swaps())
        copies = [
            pltpu.make_async_copy(
                ref.at[part, :], piece_ref.at[:, pl.ds(column * depth, depth)], sems.at[column]
            )
            for column, ref in enumerate((hidden_ref, embed_ref))
        ]
        for copy in copies:
            copy.start()
        for copy in copies:
            copy.wait()

    return kernel(
        body,
        "enter",
        [hidden, embed],
        [((height, 2 * depth), jnp.bfloat16)],
        [pltpu.SemaphoreType.DMA((2,))],
        place=pl.BlockSpec(memory_space=pl.ANY),
        vmem=ENTER_BYTES,
    )[0]


def add_squares(hidden, embed, swaps):
    rows = hidden.shape[0]
    height = rows // 2

    def body(hidden_ref, embed_ref, sums_ref):
        swapped = swaps()
        lane = lax.broadcasted_iota(jnp.int32, (height, LANES), 1)
        for half in range(2):
            total = jnp.zeros((height, LANES), jnp.float32)
            for column, ref in enumerate((hidden_ref, embed_ref)):
                wide = ref[half_rows(half, height, swapped), :].astype(jnp.float32)
                total = jnp.where(lane == column, jnp.sum(wide * wide, axis=1, keepdims=True), total)
            sums_ref[half * height : (half + 1) * height, :] = total

    return kernel(body, "add_squares", [hidden, embed], [((rows, LANES), jnp.float32)])[0]


def pack(hidden, embed, sums, other_sums, swaps):
    rows, depth = hidden.shape
    height = rows // 2

    def body(hidden_ref, embed_ref, sums_ref, other_ref, piece_ref, total_ref):
        total = sums_ref[...] + other_ref[...]
        total_ref[...] = total
        second = half_rows(1, height, swaps())
        piece_ref[:, :depth] = hidden_ref[second, :]
        piece_ref[:, depth : 2 * depth] = embed_ref[second, :]
        lane = lax.broadcasted_iota(jnp.int32, (height, LANES), 1)
        spare = jnp.zeros((height, LANES), jnp.float32)
        at = 0
        for start in range(0, rows, height):
            for column in range(2):
                rest = total[start : start + height, column : column + 1]
                for _ in range(TERMS):
                    term = rest.astype(jnp.bfloat16).astype(jnp.float32)
                    rest = rest - term
                    spare = jnp.where(lane == at, term, spare)
                    at += 1
        piece_ref[:, 2 * depth :] = spare.astype(jnp.bfloat16)

    outputs = [((height, 2 * depth + LANES), jnp.bfloat16), (sums.shape, jnp.float32)]
    return kernel(body, "pack", [hidden, embed, sums, other_sums], outputs)


def project(groups, weights, other_groups=None, takes_first=None, keeps_first=None, needed=None):
    hidden_gain, embed_gain, w_hidden, w_embed = weights
    depth, width = w_hidden.shape
    variants = [groups] if other_groups is None else [groups, other_groups]
    distinct = []
    for variant in variants:
        for array, sums, _ in variant:
            for value in (array, sums):
                if all(value is not other for other in distinct):
                    distinct.append(value)
    place = {id(array): at for at, array in enumerate(distinct)}
    total = sum(group[0].shape[0] for group in groups)
    padded = max(total, LANES)

    def squares_of(ref, low, size):
        if ref.dtype == jnp.float32:
            return [ref[low : low + size, column : column + 1] for column in range(2)]
        spare = ref[:, 2 * depth :].astype(jnp.float32)
        at = low // size * 2 * TERMS
        return [
            sum(spare[:, first + t : first + t + 1] for t in range(TERMS)) for first in (at, at + TERMS)
        ]

    def body(*refs):
        sources = refs[: len(distinct)]
        hgain_ref, egain_ref, wh_ref, we_ref, *outs, normed = refs[len(distinct) :]

        def norm(variant):
            at = 0
            for array, sums, low in variant:
                size = array.shape[0]
                squares = squares_of(sources[place[id(sums)]], low, size)
                for column, gain_ref in enumerate((hgain_ref, egain_ref)):
                    part = pl.ds(column * depth, depth)
                    value = sources[place[id(array)]][:, part].astype(jnp.float32)
                    normed[at : at + size, part] = (
                        value * inverse_rms(squares[column], D) * gain_ref[...]
                    ).astype(jnp.bfloat16)
                at += size

        def run():
            if other_groups is None:
                norm(groups)
            else:
                pl.when(takes_first())(lambda: norm(groups))
                pl.when(jnp.logical_not(takes_first()))(lambda: norm(other_groups))
            result = jnp.dot(normed[:, :depth], wh_ref[...], preferred_element_type=jnp.float32)
            result = result + jnp.dot(normed[:, depth:], we_ref[...], preferred_element_type=jnp.float32)
            result = result[:total, :].astype(jnp.bfloat16)
            if keeps_first is None:
                outs[0][...] = result
            else:
                parts = (result[: total // 2, :], result[total // 2 :, :])
                outs[0][...] = jnp.where(keeps_first(), parts[0], parts[1])
                outs[1][...] = jnp.where(keeps_first(), parts[1], parts[0])

        run() if needed is None else pl.when(needed())(run)

    sizes = [total] if keeps_first is None else [total // 2] * 2
    result = kernel(
        body,
        "project",
        [*distinct, hidden_gain, embed_gain, resident(w_hidden), resident(w_embed)],
        [((size, width), jnp.bfloat16) for size in sizes],
        [pltpu.VMEM((padded, 2 * depth), jnp.bfloat16)],
    )
    return result[0] if keeps_first is None else result


def latent_partial(own, received, gain, w_latent, cuts, known=(), route=(), needed=None):
    rows, width = own.shape
    lat = w_latent.shape[0]
    padded = -(-(lat + 2) // LANES) * LANES
    edge = padded - LANES

    def run(own_ref, received_ref, gain_ref, w_ref, *refs):
        known_refs, mtp_ref, lat_refs = refs[: len(known)], refs[len(known)], refs[len(known) + 1 :]
        mtp = (own_ref[...].astype(jnp.float32) + received_ref[...].astype(jnp.float32)).astype(
            jnp.bfloat16
        )
        mtp_ref[...] = mtp
        wide = mtp.astype(jnp.float32)
        total = jnp.sum(wide * wide, axis=1, keepdims=True)
        normed = (wide * gain_ref[...]).astype(jnp.bfloat16)
        over = (((1,), (1,)), ((), ()))
        main = lax.dot_general(
            normed, w_ref[:edge, :], over, preferred_element_type=jnp.float32
        ).astype(jnp.bfloat16)
        last = lax.dot_general(normed, w_ref[edge:, :], over, preferred_element_type=jnp.float32)
        column = lax.broadcasted_iota(jnp.int32, (rows, padded - lat), 1)
        high_half = total.astype(jnp.bfloat16).astype(jnp.float32)
        spare = jnp.where(column == 0, high_half, jnp.where(column == 1, total - high_half, 0.0))
        last = jnp.concatenate([last, spare], axis=1).astype(jnp.bfloat16)

        def put(ref, at, part):
            if part < len(known):
                ref[at : at + known[part].shape[0], :] = known_refs[part][...]
            else:
                low, high = cuts[part - len(known)]
                ref[at : at + high - low, :edge] = main[low:high, :]
                ref[at : at + high - low, edge:] = last[low:high, :]

        if not route:
            for part, ref in enumerate(lat_refs):
                put(ref, 0, part)
        for whens, ref in zip(route, lat_refs, strict=False):
            for block, when in enumerate(whens):
                for part in range(len(known) + len(cuts)):
                    pl.when(when() == part)(
                        lambda ref=ref, block=block, part=part: put(ref, block * height, part)
                    )

    def body(*refs):
        run(*refs) if needed is None else pl.when(needed())(lambda: run(*refs))

    sizes = [high - low for low, high in cuts]
    height = sizes[0]
    if route:
        sizes = [height * len(whens) for whens in route]
    outputs = [((rows, width), jnp.bfloat16)] + [((size, padded), jnp.bfloat16) for size in sizes]
    mtp, *parts = kernel(body, "latent_partial", [own, received, gain, resident(w_latent), *known], outputs)
    return mtp, parts


def add_parts(inner, outer, pairs, single, far, is_end):
    rows, width = inner.shape

    def body(inner_ref, outer_ref, first_ref, second_ref, single_ref, far_ref, base_ref, owed_ref):
        outer_sum = outer_ref[...].astype(jnp.float32) + far_ref[...].astype(jnp.float32)
        inner_sum = inner_ref[...].astype(jnp.float32) + single_ref[...].astype(jnp.float32)
        for ref in (first_ref, second_ref):
            inner_sum = inner_sum + ref[:rows, :].astype(jnp.float32)
            outer_sum = outer_sum + ref[rows:, :].astype(jnp.float32)
        base_ref[...] = jnp.where(is_end(), outer_sum, inner_sum)
        owed_ref[:, :width] = outer_sum.astype(jnp.bfloat16)
        owed_ref[:, width:] = jnp.zeros((rows, LANES), jnp.bfloat16)

    return kernel(
        body,
        "add_parts",
        [inner, outer, *pairs, single, far],
        [((rows, width), jnp.float32), ((rows, width + LANES), jnp.bfloat16)],
    )


def place_rows(choices, shape, swaps):
    height = shape[0] // 4

    def body(*refs):
        *refs, out = refs
        swapped = swaps()
        for shard, first, when, array in choices:
            terms = [refs.pop(0) for _ in (array if isinstance(array, tuple) else (array,))]
            array = array[0] if isinstance(array, tuple) else array

            @pl.when(when())
            def _(shard=shard, first=first, array=array, terms=terms):
                size = min(array.shape[0], height)
                for at in range(array.shape[0] // size):
                    half, within = (first + at, 0) if isinstance(first, int) else (1, first())
                    row = (2 * shard + half + (1 - 2 * half) * swapped) * height + within
                    value = terms[0][at * size : (at + 1) * size, :]
                    if len(terms) > 1:
                        value = value.astype(jnp.float32) + terms[1][...].astype(jnp.float32)
                    out[pl.ds(pl.multiple_of(row, size), size), :] = value.astype(jnp.bfloat16)

    inputs = []
    for choice in choices:
        inputs += choice[-1] if isinstance(choice[-1], tuple) else [choice[-1]]
    return kernel(body, "place_rows", inputs, [(shape, jnp.bfloat16)])[0]


def finish(base, late, q_gain, kv_gain, cosine, sine_grid, first_row):
    rows = base.shape[0]
    lat = Q_LAT + KV_LAT
    rope = 2 * cosine.shape[1]

    def body(base_ref, *refs):
        late_refs = refs[: len(late)]
        qg_ref, kg_ref, cos_ref, sin_ref, q_ref, kv_ref, rope_ref, total = refs[len(late) :]
        total[...] = base_ref[...]
        for (at, array), ref in zip(late, late_refs, strict=True):
            size = array.shape[0]
            total[pl.ds(pl.multiple_of(at(), size), size), :] += ref[:, : total.shape[1]].astype(jnp.float32)
        whole = total[...]
        squares = whole[:, lat + rope : lat + rope + 1] + whole[:, lat + rope + 1 : lat + rope + 2]
        latent = whole * inverse_rms(squares, D)
        q = latent[:, :Q_LAT]
        kv = latent[:, Q_LAT:lat]
        q_scale = inverse_rms(jnp.sum(q * q, axis=1, keepdims=True), Q_LAT)
        kv_scale = inverse_rms(jnp.sum(kv * kv, axis=1, keepdims=True), KV_LAT)
        q_ref[...] = (q * q_scale * qg_ref[...]).astype(jnp.bfloat16)
        kv_ref[...] = (kv * kv_scale * kg_ref[...]).astype(jnp.bfloat16)
        own = pl.ds(pl.multiple_of(first_row(), rows), rows)
        keys = rotate_keys(latent[:, lat : lat + rope], cos_ref[own, :], sin_ref[own, :])
        rope_ref[...] = keys.astype(jnp.bfloat16)

    return kernel(
        body,
        "finish",
        [base, *[array for _, array in late], q_gain, kv_gain, cosine, sine_grid],
        [((rows, Q_LAT), jnp.bfloat16), ((rows, KV_LAT), jnp.bfloat16), ((rows, rope), jnp.bfloat16)],
        [pltpu.VMEM(base.shape, jnp.float32)],
    )


def shards_line(
    hidden_in, embed_in, hidden_gain, embed_gain, w_hidden, w_embed, attn_gain, w_latent, q_gain, kv_gain
):
    line = lax.axis_size("dp")
    last = line - 1
    shard = hidden_in.shape[0]
    rows_out = shard // 2
    halves = ((0, rows_out), (rows_out, shard))

    def me():
        return lax.axis_index("dp")

    def mine():
        return lax.axis_index("mp")

    def owner(s):
        return s // 2

    def device(d, m):
        return d * 2 + m

    def to_owner(value, senders):
        pairs = [(device(d, 1 - m), device(d, m)) for d, m in senders]
        return lax.ppermute(value, ("dp", "mp"), pairs)

    def shard_of(k, d):
        return sorted({s for s in (d - k, d + k) if 0 <= s < line})

    def senders_of(k):
        return [(d, owner(s)) for d in range(line) for s in shard_of(k, d)]

    def upper():
        return jnp.where(me() >= line // 2, 1, 0)

    first_piece = enter(hidden_in, embed_in, upper)
    sums = add_squares(hidden_in, embed_in, upper)
    tokens = lax.axis_size("mp") * line * rows_out
    tables = rope_tables(
        w_latent.shape[1] - Q_LAT - KV_LAT, jnp.arange(tokens, dtype=jnp.int32) % LENGTH
    )
    small = [gain[None, :] for gain in (hidden_gain, embed_gain, attn_gain, q_gain, kv_gain)] + list(tables)
    w_latent = w_latent.T
    hidden_gain, embed_gain, attn_gain, q_gain, kv_gain, cosine, sine_grid = small
    weights = (hidden_gain, embed_gain, w_hidden, w_embed)

    other_sums = lax.ppermute(sums, "mp", [(0, 1), (1, 0)])
    second_piece, sums = pack(hidden_in, embed_in, sums, other_sums, upper)
    pieces = [first_piece, second_piece]
    sums_three = lax.ppermute(sums, "dp", [(0, last), (last, 0)])

    pairs_on = [(0, 1), (1, 0), (2, 3), (3, 2)]
    middle_on = [(1, 2), (2, 1)]
    ends_on = [(2, 3), (1, 0)]
    pair_one = [lax.ppermute(x, "dp", pairs_on) for x in pieces]
    cross_one = [lax.ppermute(x, "dp", middle_on) for x in pieces]
    ends_two = [lax.ppermute(cross_one[0], "dp", ends_on)]
    middle_two = [lax.ppermute(pair_one[0], "dp", middle_on)]
    pair_one[0], cross_one[0], sums = lax.optimization_barrier((pair_one[0], cross_one[0], sums))
    groups = [(piece, sums, low) for piece, (low, _) in zip(pieces, halves, strict=True)]
    got_own = project(groups, weights)
    pair_one[1], cross_one[1], got_own, sums_three = lax.optimization_barrier(
        (pair_one[1], cross_one[1], got_own, sums_three)
    )
    ends_two.append(lax.ppermute(cross_one[1], "dp", ends_on))
    middle_two.append(lax.ppermute(pair_one[1], "dp", middle_on))
    received_own = to_owner(got_own, senders_of(0))
    mtp_own, lat_own = latent_partial(got_own, received_own, attn_gain, w_latent, halves)

    def pair_is_own():
        return upper() == mine()

    def pair_is_other():
        return upper() != mine()

    groups_pair = [(x, pair_one[1], low) for x, (low, _) in zip(pair_one, halves, strict=True)]
    groups_cross = [(x, cross_one[1], low) for x, (low, _) in zip(cross_one, halves, strict=True)]
    received_one = to_owner(project(groups_pair, weights, groups_cross, pair_is_other), senders_of(1))
    got_one = project(groups_pair, weights, groups_cross, pair_is_own)
    middle_two[0], ends_two[0], received_one = lax.optimization_barrier(
        (middle_two[0], ends_two[0], received_one)
    )
    three = [lax.ppermute(middle_two[0], "dp", ends_on)]
    mtp_one, lat_one = latent_partial(got_one, received_one, attn_gain, w_latent, halves)
    middle_two[1], ends_two[1], lat_one, lat_own = lax.optimization_barrier(
        (middle_two[1], ends_two[1], lat_one, lat_own)
    )
    three.append(lax.ppermute(middle_two[1], "dp", ends_on))

    def is_end():
        return jnp.logical_or(me() == 0, me() == last)

    groups_ends = [(x, ends_two[1], low) for x, (low, _) in zip(ends_two, halves, strict=True)]
    groups_middle = [(x, middle_two[1], low) for x, (low, _) in zip(middle_two, halves, strict=True)]
    got_two = project(groups_ends, weights, groups_middle, is_end)
    received_two = to_owner(got_two, senders_of(2))
    sums_three = after(sums_three, got_two)
    got_three = [project([(three[0], sums_three, 0)], weights, needed=is_end)]
    received_two = after(received_two, got_three[0])

    def part_for(half, place):
        return 2 * jnp.abs(me() - (2 * mine() + half)) + jnp.where(mine() == 1, 1 - place, place)

    mtp_two, (inner, outer, away) = latent_partial(
        got_two,
        received_two,
        attn_gain,
        w_latent,
        halves,
        known=[*lat_own, *lat_one],
        route=[
            [lambda: part_for(upper(), 1 - upper())],
            [lambda: part_for(upper(), upper())],
            [lambda: part_for(1 - upper(), upper()), lambda: part_for(1 - upper(), 1 - upper())],
        ],
    )

    def send(value, pairs):
        pairs = [(device(d, m), device(to, m)) for m, d, to in pairs]
        return lax.ppermute(value, ("dp", "mp"), pairs)

    both = range(2)
    crossing = [
        send(away, [(0, 0, 2), (1, 3, 1)]),
        send(away, [(m, d, to) for m in both for d, to in ((1, 2), (2, 1))]),
    ]
    single = send(inner, [(m, d, to) for m in both for d, to in ((0, 1), (3, 2))])

    to_middle = [(0, last, 1), (1, 0, 2)]
    whole = ((0, rows_out),)
    mtp, (lat,) = latent_partial(
        got_three[0], to_owner(got_three[0], senders_of(3)), attn_gain, w_latent, whole, needed=is_end
    )
    mtp_three = [mtp]
    far = send(lat, to_middle)
    sums_three = after(sums_three, got_three[0], inner)
    part = rows_out // 2
    kept, given = project([(three[1], sums_three, rows_out)], weights, keeps_first=lambda: mine() == 0, needed=is_end)
    ends = (0, last)
    received = lax.ppermute(
        given, ("dp", "mp"), [(device(d, m), device(d, 1 - m)) for d in ends for m in range(2)]
    )
    mtp, (lat,) = latent_partial(kept, received, attn_gain, w_latent, ((0, part),), needed=is_end)
    mtp_three += [mtp, (given, to_owner(kept, [(last, 0), (0, 1)]))]
    late = [
        (lambda: part * mine(), send(lat, to_middle)),
        (
            lambda: part * (1 - mine()),
            lax.ppermute(lat, ("dp", "mp"), [(device(last, 1), device(1, 0)), (device(0, 0), device(2, 1))]),
        ),
    ]

    base, owed = add_parts(inner, outer, crossing, single, far, is_end)
    owed = send(owed, [(m, d, to) for m in both for d, to in ((1, 0), (2, last))])
    late = [(lambda: 0, owed), *late]

    def distance(offset):
        return jnp.abs(me() - (2 * mine() + offset))

    choices = []
    for offset in range(2):
        for k, mtp in enumerate((mtp_own, mtp_one, mtp_two)):
            choices.append((offset, 0, lambda offset=offset, k=k: distance(offset) == k, mtp))
        for half, mtp in zip((0, lambda: part * mine(), lambda: part * (1 - mine())), mtp_three, strict=True):
            choices.append((offset, half, lambda offset=offset: distance(offset) == last, mtp))
    mtp_hidden = place_rows(choices, (2 * shard, w_hidden.shape[1]), mine)

    q_latent, kv_latent, key_rope = finish(
        base, late, q_gain, kv_gain, cosine, sine_grid, lambda: (mine() * line + me()) * rows_out
    )
    return (mtp_hidden, q_latent, kv_latent, key_rope)


def shards_any(
    hidden_in, embed_in, hidden_gain, embed_gain, w_hidden, w_embed, attn_gain, w_latent, q_gain, kv_gain
):
    hidden_wide = hidden_in.astype(jnp.float32)
    embed_wide = embed_in.astype(jnp.float32)
    entry_sums = lax.psum(
        (jnp.sum(hidden_wide * hidden_wide, axis=1), jnp.sum(embed_wide * embed_wide, axis=1)), "mp"
    )
    hidden_norm = (hidden_wide * inverse_rms(entry_sums[0], D)[:, None] * hidden_gain[None, :]).astype(jnp.bfloat16)
    embed_norm = (embed_wide * inverse_rms(entry_sums[1], D)[:, None] * embed_gain[None, :]).astype(jnp.bfloat16)
    hidden_all = lax.all_gather(hidden_norm, "dp", axis=0, tiled=True)
    embed_all = lax.all_gather(embed_norm, "dp", axis=0, tiled=True)
    tok_share = hidden_all.shape[0] // lax.axis_size("mp")
    proj_sum = lax.psum_scatter(
        (
            jnp.dot(hidden_all, w_hidden, preferred_element_type=jnp.float32)
            + jnp.dot(embed_all, w_embed, preferred_element_type=jnp.float32)
        ).astype(jnp.bfloat16),
        "mp",
        scatter_dimension=0,
        tiled=True,
    )
    mtp_hidden = lax.optimization_barrier(proj_sum)
    proj_wide = mtp_hidden.astype(jnp.float32)
    normed_rows = (proj_wide * attn_gain[None, :]).astype(jnp.bfloat16)
    partial_latent = jnp.dot(normed_rows, w_latent, preferred_element_type=jnp.float32)
    rows_out = tok_share // lax.axis_size("dp")
    square_total = lax.psum(jnp.sum(proj_wide * proj_wide, axis=1), "dp")
    latent_sum = lax.psum_scatter(
        partial_latent.astype(jnp.bfloat16), "dp", scatter_dimension=0, tiled=True
    ).astype(jnp.float32)
    first_own = lax.axis_index("dp") * rows_out
    square_sum = lax.dynamic_slice_in_dim(square_total, first_own, rows_out, 0)
    latent = latent_sum * inverse_rms(square_sum, D)[:, None]
    first_token = lax.axis_index("mp") * tok_share + first_own
    positions = (first_token + jnp.arange(rows_out, dtype=jnp.int32)) % LENGTH
    q_latent = latent_norm(latent[:, :Q_LAT], q_gain)
    kv_latent = latent_norm(latent[:, Q_LAT : Q_LAT + KV_LAT], kv_gain)
    rope_part = latent[:, Q_LAT + KV_LAT :]
    key_rope = rotate_keys(rope_part, *rope_tables(rope_part.shape[1], positions)).astype(jnp.bfloat16)
    return (mtp_hidden, q_latent, kv_latent, key_rope)


def solution(mesh):
    placed = (
        P(("branch", "dp"), "mp"),
        P(("branch", "dp"), "mp"),
        P(("branch", "mp")),
        P(("branch", "mp")),
        P(("branch", "mp"), "dp"),
        P(("branch", "mp"), "dp"),
        P(("branch", "dp")),
        P(("branch", "dp"), None),
        P("branch"),
        P("branch"),
    )
    in_line = mesh.shape["dp"] == 4 and mesh.shape["mp"] == 2
    return jax.shard_map(
        shards_line if in_line else shards_any,
        mesh=mesh,
        in_specs=placed,
        out_specs=(
            P(("branch", "mp"), "dp"),
            P(("branch", "mp", "dp"), None),
            P(("branch", "mp", "dp"), None),
            P(("branch", "mp", "dp"), None),
        ),
        check_vma=False,
    )
```
